32 devices in a mesh: seq: 8 (over y, x, core), docs: 4 (over z).
Axes of the slice: x: 2, y: 2, z: 4, core: 2. Of those that a mesh axis runs over, the one named last changes fastest.
Arguments:
- tokens: bfloat16 [8, 2048, 768], P('docs', 'seq'), may hold values from -6 to 6
- out_grad: bfloat16 [8, 2048, 768], P('docs', 'seq'), may hold values from -6 to 6
- pool_grad: float32 [4, 768], replicated, may hold values from -768 to 768
- doc_lengths: int32 [8], P('docs'), may hold values from 512 to 2048, as said below
- prompt_mask: int32 [8, 2048], P('docs', 'seq'), may hold values from 0 to 1, as said below
- doc_groups: int32 [8], P('docs'), may hold values from 0 to 3, as said below
- bucket_ids: int32 [4095], replicated, may hold values from 0 to 31
- qkv_proj: float32 [768, 2304], P('docs'), may hold values from -0.109375 to 0.109375
- out_proj: float32 [768, 768], P('docs'), may hold values from -1.75 to 1.75
- up_proj: float32 [768, 3072], P('docs'), may hold values from -0.21875 to 0.21875
- down_proj: float32 [3072, 768], P('docs'), may hold values from -0.109375 to 0.109375
- norm_gains: float32 [768, 2], P('docs'), may hold values from 0 to 3
- bias_table: float32 [32, 12], P('docs'), may hold values from -6 to 6
- qkv_first: float32 [768, 2304], P('docs')
- out_first: float32 [768, 768], P('docs')
- up_first: float32 [768, 3072], P('docs')
- down_first: float32 [3072, 768], P('docs')
- gain_first: float32 [768, 2], P('docs')
- table_first: float32 [32, 12], P('docs')
- qkv_second: float32 [768, 2304], P('docs'), as said below
- out_second: float32 [768, 768], P('docs'), as said below
- up_second: float32 [768, 3072], P('docs'), as said below
- down_second: float32 [3072, 768], P('docs'), as said below
- gain_second: float32 [768, 2], P('docs'), as said below
- table_second: float32 [32, 12], P('docs'), as said below
Outputs:
- layer_out: bfloat16 [8, 2048, 768], P('docs', 'seq')
- pooled: float32 [4, 768], replicated
- tokens_grad: float32 [8, 2048, 768], P('docs', 'seq')
- grad_norm: float32 [], replicated
- qkv_mean: float32 [768, 2304], P('docs')
- out_mean: float32 [768, 768], P('docs')
- up_mean: float32 [768, 3072], P('docs')
- down_mean: float32 [3072, 768], P('docs')
- gain_mean: float32 [768, 2], P('docs')
- table_mean: float32 [32, 12], P('docs')
- qkv_square: float32 [768, 2304], P('docs')
- out_square: float32 [768, 768], P('docs')
- up_square: float32 [768, 3072], P('docs')
- down_square: float32 [3072, 768], P('docs')
- gain_square: float32 [768, 2], P('docs')
- table_square: float32 [32, 12], P('docs')
- qkv_next: float32 [768, 2304], P('docs')
- out_next: float32 [768, 768], P('docs')
- up_next: float32 [768, 3072], P('docs')
- down_next: float32 [3072, 768], P('docs')
- gain_next: float32 [768, 2], P('docs')
- table_next: float32 [32, 12], P('docs')
The draws below stay inside these ranges and needn't reach their ends.
Inputs may be any that keep to these rules, and one draw needn't show every extreme that they name: `doc_lengths`: among the 2 documents held by each index of docs, one has 2048 tokens. `prompt_mask`: in each document the ones form a leading run of 1 to 256 positions. `doc_groups`: every group holds at least one document. `qkv_second`: Positive. `out_second`: Positive. `up_second`: Positive. `down_second`: Positive. `gain_second`: Positive. `table_second`: Positive.
All inputs are finite; a program needn't handle non-finite values.
Results may differ from the reference program's by a relative error of at most 0.012.
The reference program's roundings to bfloat16 on the way count: a program that leaves them out, or rounds other values in their place, can miss the bound.
Values may be sent and summed in bfloat16 or wider, within the bound.
A program may use at most 320 MiB of HBM per device.

```python
import math
import jax
import jax.numpy as jnp
from jax import lax

D = 768
H = 12
DH = 64
FF = 3072
NB = 32
MB = 2
STEP = 10
LEN = 2048
SEQS = 8
GROUPS = 4


def grad_size(factor):
    return factor / math.sqrt(4 * D * D + 2 * D * FF + 2 * D + NB * H)


def first_moment(key, shape, factor):
    size = grad_size(factor) * 0.1 / 0.9
    return size * jax.random.uniform(key, shape, jnp.float32, -2.0, 2.0)


def second_moment(key, shape, factor):
    size = grad_size(factor) ** 2 * 0.05 / 0.95
    return size * jnp.exp(jax.random.uniform(key, shape, jnp.float32, 0.0, math.log(4.0)))


def draw_norm_gains(key, part):
    key = jax.random.fold_in(key, 5)
    ramp = jnp.arange(D, dtype=jnp.float32) / D - 0.5
    rise = math.log(3.0)
    noise = jax.random.uniform(key, (D, 2), jnp.float32, 0.8, 1.2)
    return jnp.exp(rise * ramp)[:, None] * noise


def draw_doc_lengths(key, part):
    key = jax.random.fold_in(key, 7)
    first_key, second_key = jax.random.split(key)
    ragged = jax.random.randint(first_key, (SEQS,), LEN // 4, LEN + 1)
    chosen = jax.random.randint(second_key, (SEQS // MB,), 0, MB)
    slot = jnp.arange(SEQS, dtype=jnp.int32) % MB
    full = slot == jnp.repeat(chosen, MB)
    return jnp.where(full, LEN, ragged).astype(jnp.int32)


def draw_prompt_mask(key, part):
    key = jax.random.fold_in(key, 8)
    prefix = jax.random.randint(key, (SEQS, 1), 1, LEN // 8 + 1)
    return (jnp.arange(LEN, dtype=jnp.int32)[None, :] < prefix).astype(jnp.int32)


def draw_doc_groups(key, part):
    key = jax.random.fold_in(key, 9)
    first_key, second_key = jax.random.split(key)
    order = jnp.arange(SEQS, dtype=jnp.int32)
    extra = jax.random.randint(first_key, (SEQS,), 0, GROUPS)
    named = jnp.where(order < GROUPS, order, extra)
    return jax.random.permutation(second_key, named).astype(jnp.int32)


def draw_qkv_first(key, part):
    key = jax.random.fold_in(key, 11)
    return first_moment(key, (D, 3 * D), 1.9)


def draw_out_first(key, part):
    key = jax.random.fold_in(key, 12)
    return first_moment(key, (D, D), 0.085)


def draw_up_first(key, part):
    key = jax.random.fold_in(key, 13)
    return first_moment(key, (D, FF), 0.25)


def draw_down_first(key, part):
    key = jax.random.fold_in(key, 14)
    return first_moment(key, (FF, D), 0.5)


def draw_gain_first(key, part):
    key = jax.random.fold_in(key, 15)
    return first_moment(key, (D, 2), 1.3)


def draw_table_first(key, part):
    key = jax.random.fold_in(key, 16)
    return first_moment(key, (NB, H), 0.6)


def draw_qkv_second(key, part):
    key = jax.random.fold_in(key, 21)
    return second_moment(key, (D, 3 * D), 1.9)


def draw_out_second(key, part):
    key = jax.random.fold_in(key, 22)
    return second_moment(key, (D, D), 0.085)


def draw_up_second(key, part):
    key = jax.random.fold_in(key, 23)
    return second_moment(key, (D, FF), 0.25)


def draw_down_second(key, part):
    key = jax.random.fold_in(key, 24)
    return second_moment(key, (FF, D), 0.5)


def draw_gain_second(key, part):
    key = jax.random.fold_in(key, 25)
    return second_moment(key, (D, 2), 1.3)


def draw_table_second(key, part):
    key = jax.random.fold_in(key, 26)
    return second_moment(key, (NB, H), 0.6)


def plant(drawn, key, least, largest):
    spot = [jax.random.randint(jax.random.fold_in(key, axis), (), 0, length) for axis, length in enumerate(drawn.shape)]
    main_axis = drawn.shape.index(max(drawn.shape))
    next_to = spot[:main_axis] + [(spot[main_axis] + 1) % drawn.shape[main_axis]] + spot[main_axis + 1:]
    return drawn.at[tuple(spot)].set(least).at[tuple(next_to)].set(largest)


def levels(stream_key, dims, cuts, smallest, largest):
    def one(position, blocks):
        draws = jax.random.uniform(jax.random.fold_in(jax.random.fold_in(stream_key, 6), position), (blocks,), jnp.float32, smallest / len(cuts), largest / len(cuts))
        return jnp.repeat(jnp.exp(draws), dims[position] // blocks).reshape((-1,) + (1,) * (len(dims) - position - 1))

    gain = one(*cuts[0])
    for cut in cuts[1:]:
        gain = gain * one(*cut)
    return gain


def bell_draw(rng, shape, deviation, limit, pieces=(), kind=jnp.bfloat16):
    level = levels(rng, shape, pieces, -0.22, 0.18) if pieces else 1.0
    entries = jax.random.normal(rng, shape, jnp.float32) * deviation * level
    return jnp.minimum(jnp.maximum(entries, -limit), limit).astype(kind)


def setup_inputs(seed: int = 0) -> dict:
    key_of = jax.random.split(jax.random.key(seed), 26)
    return {
        "tokens": bell_draw(key_of[0], (SEQS, LEN, D), 1.0, 6.0, ((0, 4), (1, 8))),
        "out_grad": bell_draw(key_of[1], (SEQS, LEN, D), 1.0, 6.0, ((0, 4), (1, 8))),
        "pool_grad": bell_draw(key_of[2], (GROUPS, D), (LEN // 16), 768.0, (), jnp.float32),
        "doc_lengths": draw_doc_lengths(jax.random.fold_in(key_of[25], 71), 0),
        "prompt_mask": draw_prompt_mask(jax.random.fold_in(key_of[25], 71), 0),
        "doc_groups": draw_doc_groups(jax.random.fold_in(key_of[25], 71), 0),
        "bucket_ids": plant(jax.random.randint(key_of[6], (2 * LEN - 1,), 0, NB), jax.random.fold_in(key_of[6], 1), 0, NB - 1).astype(jnp.int32),
        "qkv_proj": bell_draw(key_of[7], (D, 3 * D), (4 * D) ** -0.5, 0.109375, ((0, 4),), jnp.float32),
        "out_proj": bell_draw(key_of[8], (D, D), (D // 64) ** -0.5, 1.75, ((0, 4),), jnp.float32),
        "up_proj": bell_draw(key_of[9], (D, FF), D ** -0.5, 0.21875, ((0, 4),), jnp.float32),
        "down_proj": bell_draw(key_of[10], (FF, D), FF ** -0.5, 0.109375, ((0, 4),), jnp.float32),
        "norm_gains": draw_norm_gains(jax.random.fold_in(key_of[25], 71), 0),
        "bias_table": bell_draw(key_of[12], (NB, H), 1.0, 6.0, ((0, 4),), jnp.float32),
        "qkv_first": draw_qkv_first(jax.random.fold_in(key_of[25], 71), 0),
        "out_first": draw_out_first(jax.random.fold_in(key_of[25], 71), 0),
        "up_first": draw_up_first(jax.random.fold_in(key_of[25], 71), 0),
        "down_first": draw_down_first(jax.random.fold_in(key_of[25], 71), 0),
        "gain_first": draw_gain_first(jax.random.fold_in(key_of[25], 71), 0),
        "table_first": draw_table_first(jax.random.fold_in(key_of[25], 71), 0),
        "qkv_second": draw_qkv_second(jax.random.fold_in(key_of[25], 71), 0),
        "out_second": draw_out_second(jax.random.fold_in(key_of[25], 71), 0),
        "up_second": draw_up_second(jax.random.fold_in(key_of[25], 71), 0),
        "down_second": draw_down_second(jax.random.fold_in(key_of[25], 71), 0),
        "gain_second": draw_gain_second(jax.random.fold_in(key_of[25], 71), 0),
        "table_second": draw_table_second(jax.random.fold_in(key_of[25], 71), 0),
    }


EPS = 1e-06
NEG = -1000000000.0
BETA_ONE = 0.9
BETA_TWO = 0.95
ADAM_EPS = 1e-08
CLIP_NORM = 1.0
RATES = (0.03, 0.45, 0.05, 0.03, 1.0, 1.5)
DECAYS = (0.1, 0.1, 0.1, 0.1, 0.0, 0.0)
HIGH = lax.Precision.HIGHEST

@jax.custom_vjp
def low(v):
    return lax.optimization_barrier(v.astype(jnp.bfloat16)).astype(jnp.float32)

@jax.custom_vjp
def low_back(v):
    return v

def low_keep(v):
    return (low(v), None)

def low_pass(kept, grad):
    return (grad,)

def back_keep(v):
    return (v, None)

def back_low(kept, grad):
    return (low(grad),)
low.defvjp(low_keep, low_pass)
low_back.defvjp(back_keep, back_low)

def rms_scale(values_in, gain_vec):
    return values_in * lax.rsqrt(lax.optimization_barrier(jnp.mean(values_in * values_in, axis=-1, keepdims=True)) + EPS) * gain_vec

def product(left, right):
    return jnp.dot(left, right, precision=HIGH)

def adam_update(gradient, first_state, second_state, weight, rate, decay, clip):
    gradient = gradient * clip
    first_new = BETA_ONE * first_state + (1.0 - BETA_ONE) * gradient
    second_new = BETA_TWO * second_state + (1.0 - BETA_TWO) * gradient * gradient
    fix_first = 1.0 - BETA_ONE ** STEP
    fix_second = 1.0 - BETA_TWO ** STEP
    moved = first_new / fix_first / (jnp.sqrt(second_new / fix_second) + ADAM_EPS)
    return (first_new, second_new, weight - rate * (moved + decay * weight))

def sequence_layer(rows_in, length, weights):
    qkv_low, out_low, up_low, down_low, gains_low, offset_bias = weights
    attn_in = low(rms_scale(rows_in, gains_low[:, 0]))
    qkv = product(attn_in, qkv_low)
    query = low_back(low(qkv[:, :D])).reshape(LEN, H, DH)
    keys = low_back(low(qkv[:, D:2 * D])).reshape(LEN, H, DH)
    values = low_back(low(qkv[:, 2 * D:])).reshape(LEN, H, DH)
    key_index = jnp.arange(LEN, dtype=jnp.int32)
    visible = key_index < length
    block = min(512, LEN)

    def attend(first_row):
        query_rows = first_row + jnp.arange(block, dtype=jnp.int32)
        query_block = lax.dynamic_slice_in_dim(query, first_row, block, 0)
        offsets = key_index[None, :] - query_rows[:, None] + (LEN - 1)
        bias = jnp.transpose(offset_bias[offsets], (2, 0, 1))
        scores = low_back(jnp.einsum('qhd,khd->hqk', query_block, keys, precision=HIGH)) + bias
        scores = jnp.where(visible[None, None, :], scores, NEG)
        row_max = lax.optimization_barrier(jnp.max(scores, axis=-1, keepdims=True))
        expo = jnp.exp(scores - row_max)
        probs = low(expo / lax.optimization_barrier(jnp.sum(expo, axis=-1, keepdims=True)))
        return jnp.einsum('hqk,khd->qhd', probs, values, precision=HIGH)
    firsts = jnp.arange(LEN // block, dtype=jnp.int32) * block
    mixed = low_back(low(lax.map(jax.checkpoint(attend), firsts).reshape(LEN, D)))
    hidden = rows_in + low_back(product(mixed, out_low))
    ffn_in = low(rms_scale(hidden, gains_low[:, 1]))
    upper = low_back(product(ffn_in, up_low))
    active = low(jax.nn.gelu(upper, approximate=True))
    return hidden + low_back(product(active, down_low))

def reference(tokens, out_grad, pool_grad, doc_lengths, prompt_mask, doc_groups, bucket_ids, qkv_proj, out_proj, up_proj, down_proj, norm_gains, bias_table, qkv_first, out_first, up_first, down_first, gain_first, table_first, qkv_second, out_second, up_second, down_second, gain_second, table_second):
    positions = jnp.arange(LEN, dtype=jnp.int32)
    kept = jnp.logical_and(positions[None, :] < doc_lengths[:, None], prompt_mask == 0).astype(jnp.float32)
    group_hot = (doc_groups[:, None] == jnp.arange(GROUPS, dtype=jnp.int32)[None, :]).astype(jnp.float32)
    counts = product(group_hot.T, lax.optimization_barrier(jnp.sum(kept, axis=1)))
    bucket_hot = (bucket_ids[:, None] == jnp.arange(NB, dtype=jnp.int32)[None, :]).astype(jnp.float32)

    def forward(rows_all, qkv_matrix, out_matrix, up_matrix, down_matrix, gains, table):
        weights = (low(qkv_matrix), low(out_matrix), low(up_matrix), low(down_matrix), low(gains), product(bucket_hot, low(table)))

        def one_document(carry, inputs):
            return (carry, sequence_layer(inputs[0], inputs[1], weights))
        _, final = lax.scan(jax.checkpoint(one_document), jnp.zeros((), jnp.float32), (rows_all, doc_lengths))
        per_doc = jnp.einsum('sp,spd->sd', kept, final, precision=HIGH)
        return (final, product(group_hot.T, per_doc) / counts[:, None])
    (final, pooled), pull = jax.vjp(forward, tokens.astype(jnp.float32), qkv_proj, out_proj, up_proj, down_proj, norm_gains, bias_table)
    grads = pull((out_grad.astype(jnp.float32), pool_grad))
    tokens_grad = grads[0]
    weight_grads = grads[1:]
    squares = jnp.zeros((), jnp.float32)
    for gradient in weight_grads:
        squares = squares + jnp.sum(gradient * gradient)
    grad_norm = jnp.sqrt(squares)
    clip = CLIP_NORM / jnp.maximum(grad_norm, CLIP_NORM)
    states = zip(weight_grads, (qkv_first, out_first, up_first, down_first, gain_first, table_first), (qkv_second, out_second, up_second, down_second, gain_second, table_second), (qkv_proj, out_proj, up_proj, down_proj, norm_gains, bias_table), RATES, DECAYS)
    results = [adam_update(g_item, m_item, v_item, w_item, rate, decay, clip) for g_item, m_item, v_item, w_item, rate, decay in states]
    qkv_mean, qkv_square, qkv_next = results[0]
    out_mean, out_square, out_next = results[1]
    up_mean, up_square, up_next = results[2]
    down_mean, down_square, down_next = results[3]
    gain_mean, gain_square, gain_next = results[4]
    table_mean, table_square, table_next = results[5]
    layer_out = final.astype(jnp.bfloat16)
    return (layer_out, pooled, tokens_grad, grad_norm, qkv_mean, out_mean, up_mean, down_mean, gain_mean, table_mean, qkv_square, out_square, up_square, down_square, gain_square, table_square, qkv_next, out_next, up_next, down_next, gain_next, table_next)
```

```python
from functools import partial

import jax
import jax.numpy as jnp
from jax import lax
from jax.experimental import pallas as pl
from jax.experimental.pallas import tpu as pltpu
from jax.sharding import PartitionSpec as P

D = 768
H = 12
DH = 64
NB = 32
STEP = 10

EPS = 1e-06
NEG = -1000000000.0
BETA_ONE = 0.9
BETA_TWO = 0.95
ADAM_EPS = 1e-08
CLIP_NORM = 1.0
RATES = (0.03, 0.45, 0.05, 0.03, 1.0, 1.5)
DECAYS = (0.1, 0.1, 0.1, 0.1, 0.0, 0.0)
HIGH = lax.Precision.HIGHEST
F32 = jnp.float32
BF = jnp.bfloat16


def dot(left, right):
    return jnp.dot(left, right, preferred_element_type=F32)


def three(row):
    high = row.astype(BF).astype(F32)
    rest = row - high
    mid = rest.astype(BF).astype(F32)
    return high, mid, rest - mid


def extra_rows(rows, width):
    index = lax.broadcasted_iota(jnp.int32, (64, width), 0)
    block = jnp.zeros((64, width), F32)
    for place, row in enumerate(rows):
        block = jnp.where(index == place, row, block)
    return block.astype(BF)


def fill_bias(u_ref, t_ref):
    first = u_ref[0]
    for step in range(16):
        t_ref[8 * step : 8 * step + 8, :] = pltpu.roll(first, 8 * step, 1) if step else first


def keys_with_mask(k_ref, length, size):
    place = lax.broadcasted_iota(jnp.int32, (1, size), 1)
    masked = jnp.where(place < length, 0.0, NEG)
    ones = jnp.ones((1, size), F32)
    return jnp.concatenate([k_ref[...], extra_rows([masked, ones, ones, ones], size)], axis=0).T


def forward_kernel(len_ref, q_ref, k_ref, v_ref, u_ref, o_ref, of_ref, lse_ref, t_ref, ka_ref, s_ref):
    i = pl.program_id(1)
    size, qb = s_ref.shape
    kc = 256

    @pl.when(i == 0)
    def _():
        fill_bias(u_ref, t_ref)
        ka_ref[...] = keys_with_mask(k_ref, len_ref[0], size)

    ones = jnp.ones((1, qb), F32)
    query = jnp.concatenate([q_ref[...], extra_rows([ones], qb)], axis=0)
    top = jnp.full((8, qb), -3e38, F32)
    for c in range(size // kc):
        s = dot(ka_ref[c * kc : (c + 1) * kc, :], query)
        parts = []
        for b in range(kc // 128):
            start = pl.multiple_of(i * qb + size - 128 - (c * kc + b * 128), 128)
            part = s[b * 128 : (b + 1) * 128, :] + t_ref[:, pl.ds(start, qb)]
            s_ref[c * kc + b * 128 : c * kc + (b + 1) * 128, :] = part
            top = jnp.maximum(top, jnp.max(part.reshape(16, 8, qb), axis=0))
    row_max = jnp.max(top, axis=0, keepdims=True)
    total = jnp.zeros((8, qb), F32)
    out = jnp.zeros((DH, qb), F32)
    for c in range(size // kc):
        e = jnp.exp(s_ref[c * kc : (c + 1) * kc, :] - row_max)
        total = total + jnp.sum(e.reshape(kc // 8, 8, qb), axis=0)
        out = out + dot(v_ref[:, c * kc : (c + 1) * kc], e.astype(BF))
    total = jnp.sum(total, axis=0, keepdims=True)
    out = out * (1.0 / total)
    o_ref[...] = out.astype(BF)
    of_ref[...] = out
    lse_ref[0] = row_max + jnp.log(total)


def attention_forward(qkv_t, u, length, hp):
    size = qkv_t.shape[1]
    qb = 256
    return pl.pallas_call(
        forward_kernel,
        out_shape=(
            jax.ShapeDtypeStruct((hp * DH, size), BF),
            jax.ShapeDtypeStruct((hp * DH, size), F32),
            jax.ShapeDtypeStruct((hp, 1, size), F32),
        ),
        grid=(hp, size // qb),
        in_specs=[
            pl.BlockSpec(memory_space=pltpu.SMEM),
            pl.BlockSpec((DH, qb), lambda h, i: (h, i)),
            pl.BlockSpec((DH, size), lambda h, i: (hp + h, 0)),
            pl.BlockSpec((DH, size), lambda h, i: (2 * hp + h, 0)),
            pl.BlockSpec((1, 8, 2 * size), lambda h, i: (h, 0, 0)),
        ],
        out_specs=(
            pl.BlockSpec((DH, qb), lambda h, i: (h, i)),
            pl.BlockSpec((DH, qb), lambda h, i: (h, i)),
            pl.BlockSpec((1, 1, qb), lambda h, i: (h, 0, i)),
        ),
        scratch_shapes=[
            pltpu.VMEM((128, 2 * size), F32),
            pltpu.VMEM((size, 128), BF),
            pltpu.VMEM((size, qb), F32),
        ],
        compiler_params=pltpu.CompilerParams(vmem_limit_bytes=48 << 20),
        cost_estimate=pl.CostEstimate(
            flops=16 * hp * size * size * DH, bytes_accessed=8 << 20, transcendentals=hp * size * size
        ),
        name="attention_forward",
    )(length, qkv_t, qkv_t, qkv_t, u)


def backward_kernel(
    len_ref, q_ref, k_ref, v_ref, u_ref, do_ref, of_ref, lse_ref,
    dq_ref, dk_ref, dv_ref, d8_ref,
    t_ref, dt_ref, ka_ref, va_ref, dka_ref, dva_ref,
):
    i = pl.program_id(1)
    size = k_ref.shape[1]
    qb = q_ref.shape[1]
    kc = 256

    @pl.when(i == 0)
    def _():
        fill_bias(u_ref, t_ref)
        ka_ref[...] = keys_with_mask(k_ref, len_ref[0], size)
        ones = jnp.ones((1, size), F32)
        va_ref[...] = jnp.concatenate([v_ref[...], extra_rows([ones, ones, ones], size)], axis=0).T
        dt_ref[...] = jnp.zeros_like(dt_ref)
        dka_ref[...] = jnp.zeros_like(dka_ref)
        dva_ref[...] = jnp.zeros_like(dva_ref)

    ones = jnp.ones((1, qb), F32)
    grad = do_ref[...]
    delta = jnp.sum(grad.astype(F32) * of_ref[...], axis=0, keepdims=True)
    query = jnp.concatenate([q_ref[...], extra_rows([ones, *three(-lse_ref[0])], qb)], axis=0)
    grad_t = jnp.concatenate([grad, extra_rows([*three(-delta)], qb)], axis=0)
    q_rows = q_ref[...].T
    grad_rows = grad.T
    dq = jnp.zeros((DH, qb), F32)
    held = jnp.zeros((128, qb), F32)
    lanes = qb // 128
    for c in range(size // kc):
        rows = slice(c * kc, (c + 1) * kc)
        s = dot(ka_ref[rows, :], query)
        dp = dot(va_ref[rows, :], grad_t)
        probs, scores = [], []
        for b in range(kc // 128):
            block = c * (kc // 128) + b
            start = pl.multiple_of(i * qb + size - 128 - block * 128, 128)
            sub = slice(b * 128, (b + 1) * 128)
            p = jnp.exp(s[sub, :] + t_ref[:, pl.ds(start, qb)])
            ds = p * dp[sub, :]
            held = ds if block == 0 else jnp.concatenate([ds[:, :128], held[:, : qb - 128] + ds[:, 128:]], axis=1)
            top = pl.multiple_of(start + qb - 128, 128)
            dt_ref[:, pl.ds(top, 128)] += held[:, qb - 128 :]
            probs.append(p.astype(BF))
            scores.append(ds.astype(BF))
        probs = jnp.concatenate(probs, axis=0)
        scores = jnp.concatenate(scores, axis=0)
        dva_ref[rows, :] += dot(probs, grad_rows)
        dka_ref[rows, :] += dot(scores, q_rows)
        dq = dq + dot(k_ref[:, rows], scores)
    for a in range(lanes - 1):
        start = pl.multiple_of(i * qb + a * 128, 128)
        dt_ref[:, pl.ds(start, 128)] += held[:, a * 128 : (a + 1) * 128]
    dq_ref[...] = dq.astype(BF)

    @pl.when(i == pl.num_programs(1) - 1)
    def _():
        dk_ref[...] = dka_ref[...].T.astype(BF)
        dv_ref[...] = dva_ref[...].T.astype(BF)
        total = dt_ref[0:8, :]
        for step in range(1, 16):
            total = total + pltpu.roll(dt_ref[8 * step : 8 * step + 8, :], 2 * size - 8 * step, 1)
        d8_ref[0] = total


def attention_backward(qkv_t, u, length, do_t, of_t, lse, hp):
    size = qkv_t.shape[1]
    qb = 256
    return pl.pallas_call(
        backward_kernel,
        out_shape=(
            jax.ShapeDtypeStruct((hp * DH, size), BF),
            jax.ShapeDtypeStruct((hp * DH, size), BF),
            jax.ShapeDtypeStruct((hp * DH, size), BF),
            jax.ShapeDtypeStruct((hp, 8, 2 * size), F32),
        ),
        grid=(hp, size // qb),
        in_specs=[
            pl.BlockSpec(memory_space=pltpu.SMEM),
            pl.BlockSpec((DH, qb), lambda h, i: (h, i)),
            pl.BlockSpec((DH, size), lambda h, i: (hp + h, 0)),
            pl.BlockSpec((DH, size), lambda h, i: (2 * hp + h, 0)),
            pl.BlockSpec((1, 8, 2 * size), lambda h, i: (h, 0, 0)),
            pl.BlockSpec((DH, qb), lambda h, i: (h, i)),
            pl.BlockSpec((DH, qb), lambda h, i: (h, i)),
            pl.BlockSpec((1, 1, qb), lambda h, i: (h, 0, i)),
        ],
        out_specs=(
            pl.BlockSpec((DH, qb), lambda h, i: (h, i)),
            pl.BlockSpec((DH, size), lambda h, i: (h, 0)),
            pl.BlockSpec((DH, size), lambda h, i: (h, 0)),
            pl.BlockSpec((1, 8, 2 * size), lambda h, i: (h, 0, 0)),
        ),
        scratch_shapes=[
            pltpu.VMEM((128, 2 * size), F32),
            pltpu.VMEM((128, 2 * size), F32),
            pltpu.VMEM((size, 128), BF),
            pltpu.VMEM((size, 128), BF),
            pltpu.VMEM((size, DH), F32),
            pltpu.VMEM((size, DH), F32),
        ],
        compiler_params=pltpu.CompilerParams(vmem_limit_bytes=48 << 20),
        cost_estimate=pl.CostEstimate(
            flops=40 * hp * size * size * DH, bytes_accessed=12 << 20, transcendentals=hp * size * size
        ),
        name="attention_backward",
    )(length, qkv_t, qkv_t, qkv_t, u, do_t, of_t, lse)


MESH = pl.DeviceIdType.MESH


def flip(index, bit):
    return index + bit - 2 * bit * lax.rem(lax.div(index, bit), 2)


def remote(src, dst, send_sem, recv_sem, seq, docs):
    return pltpu.make_async_remote_copy(
        src_ref=src,
        dst_ref=dst,
        send_sem=send_sem,
        recv_sem=recv_sem,
        device_id={"seq": seq, "docs": docs},
        device_id_type=MESH,
    )


def greet_signal(seq_size, docs_size):
    me, zi = lax.axis_index("seq"), lax.axis_index("docs")
    barrier = pltpu.get_barrier_semaphore()
    for step in range(1, seq_size):
        pl.semaphore_signal(
            barrier, inc=1, device_id={"seq": lax.rem(me + step, seq_size), "docs": zi}, device_id_type=MESH
        )
    for step in range(1, docs_size):
        pl.semaphore_signal(
            barrier, inc=1, device_id={"seq": me, "docs": lax.rem(zi + step, docs_size)}, device_id_type=MESH
        )


def greet_wait(seq_size, docs_size):
    pl.semaphore_wait(pltpu.get_barrier_semaphore(), seq_size + docs_size - 2)


def piece(kind, ref, first, count, owner):
    where = pl.ds(first, count)
    if kind == "rows":
        return ref.at[where, lax.div(owner, 2)]
    _, rows, columns = ref.shape
    if kind == "columns":
        width = columns // 4
        return ref.at[where, :, pl.ds(pl.multiple_of(lax.div(owner, 2) * width, 128), width)]
    height, width = rows // 4, columns // 2
    return ref.at[
        where,
        pl.ds(pl.multiple_of(lax.div(owner, 2) * height, 16), height),
        pl.ds(pl.multiple_of(lax.rem(owner, 2) * width, 128), width),
    ]


KINDS = ("both", "columns", "rows")


def front_kernel(
    hp,
    len_ref, group_ref, tokens_ref, mask_ref, back_ids_ref, gains_ref, table_ref, qkv_proj, out_proj, up_proj, down_proj,
    mixed_ref, attn_ref, qkv_ref, of_ref, lse_ref, strip_ref, ids_ref, w_ref, out_all, up_all, down_all, gain_out, count_out,
    x_s, attn_s, w_s, qkv_s, small_s, smallf_s, turn_s, plane_s, column_s, o_s, of_s, t_ref, ka_ref, s_ref, s2_ref,
    window_s, outf_s, upf_s, downf_s, out_s, up_s, down_s,
    tok_send, tok_recv, w_send, w_recv, small_send, small_recv, plane_send, plane_recv, column_send, column_recv,
    mix_send, mix_recv, z_send, z_recv, c_send, c_recv, p_send, p_recv, keep_sem, load_sem,
):
    me, zi = lax.axis_index("seq"), lax.axis_index("docs")
    n, docs = 8, small_s.shape[0]
    rows = tokens_ref.shape[1]
    size = ids_ref.shape[1] // 2
    shard = qkv_proj.shape[0]
    side = shard // 2
    table_rows = NB // docs
    chip, core, up_bit = lax.div(me, 2), lax.rem(me, 2), lax.div(me, 4)
    sibling, beside, above = flip(me, 1), flip(me, 2), flip(me, 4)
    corner = flip(beside, 4)
    my_doc, my_heads = lax.div(me, 4), lax.rem(me, 4)
    alls, shards = (out_all, up_all, down_all), (out_s, up_s, down_s)
    def z_of(k):
        return (zi, flip(zi, 1), flip(zi, 2), flip(flip(zi, 1), 2))[k]

    fulls, masters = (outf_s, upf_s, downf_s), (out_proj, up_proj, down_proj)

    def doc_slot(owner):
        return x_s.at[pl.ds(pl.multiple_of(owner * rows, rows), rows), :]

    def w_side(z, which):
        return w_s.at[pl.ds(pl.multiple_of(z * shard + which * side, 16), side), :]

    def tok_copy(slot, owner=None):
        if slot == 0:
            return remote(tokens_ref.at[1 - my_doc], doc_slot(me), tok_send.at[0], tok_recv.at[me], above, zi)
        src = tokens_ref.at[my_doc] if slot == 1 else doc_slot(owner)
        owner = me if slot == 1 else owner
        return remote(src, doc_slot(owner), tok_send.at[slot], tok_recv.at[owner], beside, zi)

    def tok_pass(owner, k):
        return remote(doc_slot(owner), doc_slot(owner), tok_send.at[4 + k], tok_recv.at[owner], sibling, zi)

    def tok_arrival(owner):
        return remote(doc_slot(owner), doc_slot(owner), tok_send.at[0], tok_recv.at[owner], sibling, zi)

    def w_copy(k):
        there = w_side(zi, up_bit)
        return remote(there, there, w_send.at[k], w_recv.at[zi], me, z_of(k))

    def w_pass(k):
        z = z_of(k)
        there = w_side(z, up_bit)
        return remote(there, there, w_send.at[docs + k], w_recv.at[docs + z], above, zi)

    def w_arrival(k, passed):
        z = z_of(k)
        there = w_side(z, 1 - up_bit if passed else up_bit)
        return remote(there, there, w_send.at[0], w_recv.at[docs + z if passed else z], above, zi)

    def small_copy(k):
        return remote(small_s.at[zi], small_s.at[zi], small_send.at[k], small_recv.at[zi], me, z_of(k))

    def small_arrival(k):
        z = z_of(k)
        return remote(small_s.at[z], small_s.at[z], small_send.at[0], small_recv.at[z], me, z)

    def plane_copy(k):
        return remote(plane_s.at[me], plane_s.at[me], plane_send.at[k], plane_recv.at[me], lax.rem(me + k, n), zi)

    def plane_arrival(k):
        owner = lax.rem(me + k, n)
        return remote(plane_s.at[owner], plane_s.at[owner], plane_send.at[0], plane_recv.at[owner], owner, zi)

    def column_copy(k):
        return remote(column_s.at[zi], column_s.at[zi], column_send.at[k], column_recv.at[zi], me, z_of(k))

    def column_arrival(k):
        z = z_of(k)
        return remote(column_s.at[z], column_s.at[z], column_send.at[0], column_recv.at[z], me, z)

    def load(j):
        if j == 0:
            return [pltpu.make_async_copy(masters[0], fulls[0], load_sem.at[0])]
        if j == 2:
            count = fulls[2].shape[0]
            here = pl.ds(pl.multiple_of(core * count, 16), count)
            return [pltpu.make_async_copy(masters[2].at[here, :], fulls[2], load_sem.at[2])]
        width = fulls[1].shape[1] // 4
        return [
            pltpu.make_async_copy(
                masters[1].at[:, pl.ds(pl.multiple_of((2 * k + core) * width, 128), width)],
                fulls[1].at[:, pl.ds(k * width, width)],
                load_sem.at[6 + k],
            )
            for k in range(4)
        ]

    def window(p):
        first = p * D + my_heads * hp * DH - DH * lax.rem(my_heads, 2)
        return pltpu.make_async_copy(
            qkv_proj.at[:, pl.ds(pl.multiple_of(first, 128), 256)], window_s.at[p], load_sem.at[3 + p]
        )

    def own_copy(j):
        return pltpu.make_async_copy(shards[j].at[0], alls[j].at[zi], keep_sem.at[j])

    def block(j, k, owner):
        return piece(KINDS[j], alls[j], z_of(k), 1, owner).at[0]

    def z_copy(j, k):
        return remote(
            piece(KINDS[j], shards[j], 0, 1, me).at[0], block(j, 0, me), z_send.at[j, k], z_recv.at[j, zi],
            me, z_of(k),
        )

    def corner_by_z(j, k):
        return j < 2 or k == 1

    def corner_copy(j, k):
        src = piece(KINDS[j], shards[j], 0, 1, corner).at[0]
        return remote(src, block(j, 0, corner), c_send.at[j, k], c_recv.at[j, zi], me, z_of(k))

    def corner_arrival(j, k):
        there = block(j, k, corner)
        return remote(there, there, c_send.at[j, k], c_recv.at[j, z_of(k)], me, zi)

    def z_arrival(j, k):
        there = block(j, k, me)
        return remote(there, there, z_send.at[j, 0], z_recv.at[j, z_of(k)], me, zi)

    def p_copy(j, k, slot):
        owner, target = (
            (me, beside), (me, above), ((above, beside), (beside, above))[(j + k) % 2], (me, sibling),
            (beside, sibling), (above, sibling), (corner, sibling),
        )[slot]
        there = block(j, k, owner)
        return remote(there, there, p_send.at[j, k, slot], p_recv.at[j, k, slot], target, zi)

    def p_arrive(j, k, *slots):
        for slot in slots:
            owner = (beside, above, corner, sibling, flip(beside, 1), flip(above, 1), flip(corner, 1))[slot]
            there = block(j, k, owner)
            remote(there, there, p_send.at[j, k, slot], p_recv.at[j, k, slot], sibling, zi).wait_recv()

    def z_finish(j):
        for k in range(1, docs):
            z_arrival(j, k).wait_recv()
            for slot in (0, 1, 3) if j == 0 else (0, 1):
                p_copy(j, k, slot).start()

    def second_start(j):
        for k in range(1, docs):
            p_arrive(j, k, 0, 1)
            for slot in (() if corner_by_z(j, k) else (2,)) + ((4, 5) if j == 0 else ()):
                p_copy(j, k, slot).start()

    def third_start(j):
        for k in range(1, docs):
            if corner_by_z(j, k):
                corner_arrival(j, k).wait_recv()
            else:
                p_arrive(j, k, 2)
            if j == 0:
                p_copy(j, k, 6).start()

    greet_signal(n, docs)
    for p in range(3):
        window(p).start()
    for j in range(3):
        for copy in load(j):
            copy.start()
    own_rows = pltpu.make_async_copy(tokens_ref.at[my_doc], doc_slot(me), keep_sem.at[3])
    own_rows.start()

    turn_s[...] = jnp.zeros_like(turn_s)
    turn_s[0:table_rows, 0:H] = table_ref[...]
    smallf_s[zi] = jnp.zeros(smallf_s.shape[1:], F32)
    smallf_s[zi, 0:2, 0:shard] = gains_ref[...]
    smallf_s[zi, 2 : 2 + H, :] = turn_s[...].T[0:H, :]
    small_s[zi] = smallf_s[zi].astype(BF)
    lane = lax.broadcasted_iota(jnp.int32, plane_s.shape[1:], 1)
    place = me * rows + lax.broadcasted_iota(jnp.int32, (1, rows), 1)
    count = jnp.zeros(plane_s.shape[1:], F32)
    for b in range(tokens_ref.shape[0]):
        kept = jnp.logical_and(place < len_ref[b], mask_ref[b : b + 1, :] == 0)
        count = count + jnp.where(lane == group_ref[b], jnp.sum(kept.astype(F32)), 0.0)
    plane_s[me] = count

    odd = lax.rem(my_heads, 2)
    for p in range(3):
        window(p).wait()
    w_own = jnp.concatenate(
        [jnp.where(odd == 1, window_s[p][:, DH:], window_s[p][:, : hp * DH]) for p in range(3)], axis=1
    )
    w_s[pl.ds(pl.multiple_of(zi * shard, 16), shard), :] = w_own.astype(BF)
    greet_wait(n, docs)
    for k in range(1, docs):
        small_copy(k).start()
        w_copy(k).start()
    tok_copy(0).start()
    tok_copy(1).start()
    for j in range(2):
        for copy in load(j):
            copy.wait()
        shards[j][0] = fulls[j][...].astype(BF)
        for k in range(1, docs):
            z_copy(j, k).start()
    for k in range(1, n):
        plane_copy(k).start()
    own_rows.wait()
    tok_pass(me, 0).start()
    load(2)[0].wait()
    shards[2][0] = fulls[2][...].astype(BF).reshape(shards[2].shape[1:])
    for j in range(3):
        own_copy(j).start()

    back_ids = jnp.broadcast_to(back_ids_ref[...], (8, 2 * size))
    index = lax.broadcasted_iota(jnp.int32, (8, 2 * size), 0)
    ids = back_ids
    for r in range(8):
        ids = jnp.where(index == r, pltpu.roll(back_ids, 2 * size + r - 127, 1), ids)
    ids_ref[...] = ids

    for k in range(1, docs):
        small_arrival(k).wait_recv()
    gain = jnp.zeros((8, D), F32)
    for z in range(docs):
        row = lax.broadcasted_iota(jnp.int32, (small_s.shape[2], D), 0)
        column = lax.broadcasted_iota(jnp.int32, (small_s.shape[2], D), 1)
        gain = gain + dot(small_s[z], (column == row + z * shard).astype(BF))[0:8, :]
        smallf_s[z] = small_s[z].astype(F32)

    gain_out[...] = gain
    gain = gain[0:1, :]

    def norm_block(owner):
        here = pl.ds(pl.multiple_of(owner * rows, rows), rows)
        values = x_s[here, :].astype(F32)
        scale = lax.rsqrt(jnp.mean(values * values, axis=-1, keepdims=True) + EPS)
        attn_s[here, :] = (values * scale * gain).astype(BF)

    norm_block(me)

    for h in range(hp):
        strip = jnp.zeros((8, 2 * size), F32)
        for z in range(docs):
            values = smallf_s[z, pl.ds(2 + my_heads * hp + h, 1), :]
            for b in range(table_rows):
                strip = jnp.where(ids == z * table_rows + b, values[:, b : b + 1], strip)
        strip_ref[h] = strip

    for k in range(1, docs):
        w_arrival(k, False).wait_recv()
        w_pass(k).start()
    for k, owner in ((1, above), (2, beside), (3, corner)):
        tok_arrival(owner).wait_recv()
        if k == 1:
            tok_copy(2, above).start()
        tok_pass(owner, k).start()
        norm_block(owner)
    for k in range(1, docs):
        z_copy(2, k).start()
    for j in range(3):
        for k in range(1, docs):
            if corner_by_z(j, k):
                corner_copy(j, k).start()
    for owner in (sibling, flip(above, 1), flip(beside, 1), flip(corner, 1)):
        tok_arrival(owner).wait_recv()
        norm_block(owner)
    keep_attn = pltpu.make_async_copy(attn_s, attn_ref, keep_sem.at[3])
    keep_attn.start()

    for k in range(1, docs):
        w_arrival(k, True).wait_recv()
    keep_w = pltpu.make_async_copy(w_s, w_ref, keep_sem.at[4])
    keep_w.start()

    @pl.loop(0, size // (2 * rows))
    def _(b):
        here = pl.ds(pl.multiple_of(b * 2 * rows, 2 * rows), 2 * rows)
        qkv_s[:, here] = dot(attn_s[here, :], w_s[...]).astype(BF).T

    keep_qkv = pltpu.make_async_copy(qkv_s, qkv_ref, keep_sem.at[5])
    keep_qkv.start()

    qb = s_ref.shape[1]
    kc = 512
    blocks = size // qb
    my_length = len_ref[my_doc]

    def mix_copy(h, i):
        src = o_s.at[pl.ds(pl.multiple_of(h * DH, DH), DH), pl.ds(pl.multiple_of(i * qb, qb), qb)]
        dst = mixed_ref.at[my_doc, pl.ds(pl.multiple_of((my_heads * hp + h) * DH, DH), DH), :]
        return src, dst

    def mix_send_copy(h, i):
        src, dst = mix_copy(h, i)
        return remote(src, dst, mix_send.at[h * n + i], mix_recv.at[me * hp + h], i, zi)

    def mix_keep_copy(h):
        src, dst = mix_copy(h, me)
        return pltpu.make_async_copy(src, dst, mix_send.at[h * n + me])

    def counts_step():
        for k in range(1, n):
            plane_arrival(k).wait_recv()
        total = plane_s[0]
        for k in range(1, n):
            total = total + plane_s[k]
        column_s[zi] = total
        for k in range(1, docs):
            column_copy(k).start()

    def events(t):
        for when, what in (
            (1, lambda: z_finish(0)),
            (2, lambda: z_finish(1)),
            (5, counts_step),
            (8, lambda: second_start(0)),
            (10, lambda: z_finish(2)),
            (18, lambda: second_start(2)),
        ):

            @pl.when(t == when)
            def _(what=what):
                what()

    def prepare(t):
        h = lax.div(t, blocks)

        @pl.when(lax.rem(t, blocks) == 0)
        def _():
            first = strip_ref[h]
            for step in range(16):
                t_ref[8 * step : 8 * step + 8, :] = pltpu.roll(first, 8 * step, 1) if step else first
            place = lax.broadcasted_iota(jnp.int32, (1, size), 1)
            masked = jnp.where(place < my_length, 0.0, NEG)
            keys = qkv_s[pl.ds(pl.multiple_of((hp + h) * DH, DH), DH), :]
            ka_ref[...] = jnp.concatenate([keys, extra_rows([masked], size)], axis=0).T

    def places(t):
        h, i = lax.div(t, blocks), lax.rem(t, blocks)
        return h, i, pl.ds(pl.multiple_of(h * DH, DH), DH), pl.ds(pl.multiple_of(i * qb, qb), qb)

    def work(ahead, behind):
        if ahead is not None:
            t, s_next = ahead
            h, i, mine_rows, here = places(t)
            query = jnp.concatenate([qkv_s[mine_rows, here], extra_rows([jnp.ones((1, qb), F32)], qb)], axis=0)
            top = jnp.full((8, qb), -3e38, F32)
        if behind is not None:
            u, s_now = behind
            hu, iu, rows_now, here_now = places(u)
            value_rows = pl.ds(pl.multiple_of((2 * hp + hu) * DH, DH), DH)
            row_max = s_now[size : size + 1, :]
            total = jnp.zeros((8, qb), F32)
            out = jnp.zeros((DH, qb), F32)
        for c in range(size // kc):
            if ahead is not None:
                scores = dot(ka_ref[c * kc : (c + 1) * kc, :], query)
                for b in range(kc // 128):
                    first = c * kc + b * 128
                    start = pl.multiple_of(i * qb + size - 128 - first, 128)
                    part = scores[b * 128 : (b + 1) * 128, :] + t_ref[:, pl.ds(start, qb)]
                    s_next[first : first + 128, :] = part
                    top = jnp.maximum(top, jnp.max(part.reshape(16, 8, qb), axis=0))
            if behind is not None:
                e = jnp.exp(s_now[c * kc : (c + 1) * kc, :] - row_max)
                total = total + jnp.sum(e.reshape(kc // 8, 8, qb), axis=0)
                out = out + dot(qkv_s[value_rows, c * kc : (c + 1) * kc], e.astype(BF))
        if ahead is not None:
            s_next[size : size + 8, :] = jnp.broadcast_to(jnp.max(top, axis=0, keepdims=True), (8, qb))
        if behind is not None:
            total = jnp.sum(total, axis=0, keepdims=True)
            out = out * (1.0 / total)
            o_s[rows_now, here_now] = out.astype(BF)
            of_s[rows_now, here_now] = out
            lse_ref[pl.ds(hu, 1), :, here_now] = (row_max + jnp.log(total)).reshape(1, 1, qb)

            @pl.when(iu != me)
            def _():
                mix_send_copy(hu, iu).start()

            @pl.when(iu == me)
            def _():
                mix_keep_copy(hu).start()

    last = hp * blocks - 1
    prepare(jnp.int32(0))
    work((jnp.int32(0), s_ref), None)

    @pl.loop(0, last // 2)
    def _(pair):
        for step, (here, there) in enumerate(((s_ref, s2_ref), (s2_ref, s_ref))):
            t = 2 * pair + step
            events(t)
            prepare(t + 1)
            work((t + 1, there), (t, here))

    events(jnp.int32(last - 1))
    work((jnp.int32(last), s2_ref), (jnp.int32(last - 1), s_ref))
    events(jnp.int32(last))
    work(None, (jnp.int32(last), s2_ref))

    keep_of = pltpu.make_async_copy(of_s, of_ref, keep_sem.at[6])
    keep_of.start()
    for k in range(1, docs):
        column_arrival(k).wait_recv()
    counts = column_s[0]
    for z in range(1, docs):
        counts = counts + column_s[z]
    count_out[...] = counts
    third_start(0)
    second_start(1)
    third_start(1)
    third_start(2)
    for j in range(3):
        own_copy(j).wait()
        for k in range(1, docs):
            if j == 0:
                p_arrive(j, k, 3, 4, 5, 6)
            z_copy(j, k).wait_send()
            for slot in range(7 if j == 0 else 3):
                if slot != 2 or not corner_by_z(j, k):
                    p_copy(j, k, slot).wait_send()
            if corner_by_z(j, k):
                corner_copy(j, k).wait_send()
    for k in range(1, docs):
        w_copy(k).wait_send()
        w_pass(k).wait_send()
        small_copy(k).wait_send()
        column_copy(k).wait_send()
    for k in range(1, n):
        plane_copy(k).wait_send()
    for k in range(4):
        tok_pass(me, k).wait_send()
    for slot in range(3):
        tok_copy(slot, above).wait_send()

    @pl.loop(0, hp * blocks)
    def _(t):
        h, i = lax.div(t, blocks), lax.rem(t, blocks)

        @pl.when(i != me)
        def _():
            mix_send_copy(h, i).wait_send()
            dst = mixed_ref.at[
                lax.div(i, 4), pl.ds(pl.multiple_of((lax.rem(i, 4) * hp + h) * DH, DH), DH), :
            ]
            remote(dst, dst, mix_send.at[h * n + i], mix_recv.at[i * hp + h], i, zi).wait_recv()

        @pl.when(i == me)
        def _():
            mix_keep_copy(h).wait()

    keep_attn.wait()
    keep_w.wait()
    keep_qkv.wait()
    keep_of.wait()


def front(lengths, groups, tokens, mask, back_ids, gains, table, masters, hp, docs):
    batches, rows, _ = tokens.shape
    size = back_ids.shape[1] // 2
    qb = 256
    width = 3 * hp * DH
    anywhere, vmem = pl.BlockSpec(memory_space=pl.ANY), pl.BlockSpec(memory_space=pltpu.VMEM)
    smem = pl.BlockSpec(memory_space=pltpu.SMEM)
    dma = pltpu.SemaphoreType.DMA
    shape = jax.ShapeDtypeStruct
    shard = gains.shape[1]
    half = (shard, masters[2].shape[1] // 2), (masters[3].shape[0] // 2, D)
    weights = [(1,) + masters[1].shape, (1,) + half[0], (1, 4, half[1][0] // 4, D)]
    return pl.pallas_call(
        partial(front_kernel, hp),
        out_shape=(
            shape((batches, H * DH, rows), BF),
            shape((size, D), BF),
            shape((width, size), BF),
            shape((hp * DH, size), F32),
            shape((hp, 1, size), F32),
            shape((hp, 8, 2 * size), F32),
            shape((8, 2 * size), jnp.int32),
            shape((D, width), BF),
            *(shape((docs,) + one[1:], BF) for one in weights),
            shape((8, D), F32),
            shape((8, 128), F32),
        ),
        in_specs=[smem, smem, anywhere, vmem, vmem, vmem, vmem] + [anywhere] * 4,
        out_specs=(anywhere,) * 4 + (vmem, vmem, vmem) + (anywhere,) * 4 + (vmem, vmem),
        scratch_shapes=[
            pltpu.VMEM((size, D), BF),
            pltpu.VMEM((size, D), BF),
            pltpu.VMEM((D, width), BF),
            pltpu.VMEM((width, size), BF),
            pltpu.VMEM((docs, 16, 256), BF),
            pltpu.VMEM((docs, 16, 256), F32),
            pltpu.VMEM((256, 128), F32),
            pltpu.VMEM((8, 8, 128), F32),
            pltpu.VMEM((docs, 8, 128), F32),
            pltpu.VMEM((hp * DH, size), BF),
            pltpu.VMEM((hp * DH, size), F32),
            pltpu.VMEM((128, 2 * size), F32),
            pltpu.VMEM((size, 128), BF),
            pltpu.VMEM((size + 8, qb), F32),
            pltpu.VMEM((size + 8, qb), F32),
            pltpu.VMEM((3, shard, 256), F32),
            *(pltpu.VMEM(one, F32) for one in (masters[1].shape, *half)),
            *(pltpu.VMEM(one, BF) for one in weights),
            dma((8,)), dma((8,)),
            dma((2 * docs,)), dma((2 * docs,)),
            dma((docs,)), dma((docs,)),
            dma((8,)), dma((8,)),
            dma((docs,)), dma((docs,)),
            dma((8 * hp,)), dma((8 * hp,)),
            dma((3, docs)), dma((3, docs)),
            dma((3, docs)), dma((3, docs)),
            dma((3, docs, 7)), dma((3, docs, 7)),
            dma((8,)), dma((10,)),
        ],
        compiler_params=pltpu.CompilerParams(
            collective_id=0, has_side_effects=True, vmem_limit_bytes=60 << 20
        ),
        name="front",
    )(lengths, groups, tokens, mask, back_ids, gains, table, *masters)


def add_to(dst, src):
    dst[...] = (dst[...].astype(F32) + src[...].astype(F32)).astype(BF)


def turned(left, right):
    return lax.dot_general(left, right, (((1,), (1,)), ((), ())), preferred_element_type=F32)


CURVE = 0.7978845608028654
CUBIC = 0.044715


def back_kernel(
    hp,
    len_ref, group_ref, mixed_ref, tokens_ref, out_grad_ref, pool_grad_ref, mask_ref, count_ref, gain_ref,
    out_all, up_all, down_all, qkv_ref, of_ref, lse_ref, strip_ref, ids_ref, attn_ref, w_ref,
    layer_ref, tokens_grad_ref, out_sum, up_sum, down_sum, qkv_sum, vec_out,
    out_s, up_s, down_s, mixed_s, gm_s, tokens_s, grad_s, ffn_s, pair_s, tmp_s, active_s, upper_s, hidden_s, final_s,
    do_s, dqkv_s, t_ref, dt_ref, ka_ref, va_ref, dka_ref, dva_ref, attn_s, w_s, qkv_s, of_s,
    one0, two0, two1, two2, three0, three1, three2, four0, four2, zf_s, fin0, fin1, fin2,
    dxr_s, dxi_s, dw_s, dwr_s, dwz_s, dwf_s, rows_s, sq_s, plane_s, column_s, tinyp_s, tinyc_s,
    load_sem, mix_send, mix_recv, keep_sem, f_send, f_recv, a_send, a_recv, b_send, b_recv, zf_send, zf_recv, z_send, z_recv, p_send, p_recv,
    x_send, x_recv, w_send, w_recv, q_send, q_recv,
    plane_send, plane_recv, column_send, column_recv, tp_send, tp_recv, tc_send, tc_recv,
):
    me, zi = lax.axis_index("seq"), lax.axis_index("docs")
    n, docs = 8, out_s.shape[0]
    half = docs // 2
    size = qkv_ref.shape[1]
    batches, rows, _ = tokens_ref.shape
    chip, core, up_bit = lax.div(me, 2), lax.rem(me, 2), lax.div(me, 4)
    sibling, beside, above = flip(me, 1), flip(me, 2), flip(me, 4)
    corner = flip(beside, 4)
    my_doc, my_heads = lax.div(me, 4), lax.rem(me, 4)
    grads, sums = (out_s, up_s, down_s), (out_sum, up_sum, down_sum)
    two = (two0, two1, two2)
    three_s, four, fin = (three0, three1, three2), (four0, None, four2), (fin0, fin1, fin2)
    chip_of = {"me": chip, "beside": lax.div(beside, 2), "above": lax.div(above, 2), "corner": lax.div(corner, 2)}

    def mix_dst(h, owner):
        return do_s.at[
            pl.ds(pl.multiple_of(h * DH, DH), DH), pl.ds(pl.multiple_of(owner * rows, rows), rows)
        ]

    def mix_src(h, target):
        first = pl.multiple_of((lax.rem(target, 4) * hp + h) * DH, DH)
        return gm_s.at[lax.div(target, 4), pl.ds(first, DH), :]

    def mix_copy(h, k):
        target = lax.rem(me + k, n)
        return remote(mix_src(h, target), mix_dst(h, me), mix_send.at[h, k], mix_recv.at[h, me], target, zi)

    def mix_keep(h):
        return pltpu.make_async_copy(mix_src(h, me), mix_dst(h, me), mix_send.at[h, 0])

    def mix_arrival(h, k):
        owner = lax.rem(me + k, n)
        return remote(mix_dst(h, owner), mix_dst(h, owner), mix_send.at[h, 0], mix_recv.at[h, owner], owner, zi)

    def acc(j, k, z, count=1):
        return piece(KINDS[j], grads[j], z, count, 2 * k + core)

    def a_copy(k):
        src = piece(KINDS[0], out_s, 0, docs, 2 * k + 1 - core)
        return remote(src, one0.at[k], a_send.at[k], a_recv.at[k], sibling, zi)

    def part(j, which, number):
        return acc(j, chip_of[which], number * half, half)

    def b_copy(j, slot):
        which, number, target = (
            ("above", 0, above), ("corner", 0, above), ("beside", 1, beside), ("corner", 1, beside),
            ("beside", 0, beside), ("above", 1, above),
        )[slot]
        dst = two[j].at[slot] if slot < 4 else three_s[j].at[slot - 4]
        return remote(part(j, which, number), dst, b_send.at[j, slot], b_recv.at[j, slot], target, zi)

    def add_parts(j, pairs):
        for (which, number), src in pairs:
            for z in range(half):
                add_to(acc(j, chip_of[which], number * half + z).at[0], src.at[z])

    def b_first():
        for k in range(4):
            a_copy(k).wait_recv()

        @pl.loop(0, 4 * docs)
        def _(step):
            k, z = lax.div(step, docs), lax.rem(step, docs)
            add_to(acc(0, k, z).at[0], one0.at[k, z])

        for slot in range(4):
            b_copy(0, slot).start()

    def b_second(j):
        for slot in range(4):
            b_copy(j, slot).wait_recv()
        add_parts(j, [(("beside", 0), two[j].at[1]), (("above", 1), two[j].at[3])])
        for slot in (4, 5):
            b_copy(j, slot).start()
        add_parts(j, [(("me", 0), two[j].at[0]), (("me", 1), two[j].at[2])])

    def z_copy(j, k):
        z = lax.rem(zi + k, docs)
        return remote(acc(j, chip, z).at[0], four[j].at[zi], z_send.at[j, k], z_recv.at[j, zi], me, z)

    def z_arrival(j, k):
        z = lax.rem(zi + k, docs)
        return remote(four[j].at[z], four[j].at[z], z_send.at[j, 0], z_recv.at[j, z], me, z)

    def z_start(j):
        for slot in (4, 5):
            b_copy(j, slot).wait_recv()
        add_parts(j, [(("me", 0), three_s[j].at[0]), (("me", 1), three_s[j].at[1])])
        for k in range(1, docs):
            z_copy(j, k).start()

    def z_of(k):
        return (zi, flip(zi, 1), flip(zi, 2), flip(flip(zi, 1), 2))[k]

    def zf_copy(c, k):
        columns = slice(c * D, (c + 1) * D)
        return remote(
            up_s.at[z_of(k), :, columns], zf_s.at[zi, :, columns], zf_send.at[c, k], zf_recv.at[c, zi], me, z_of(k)
        )

    def zf_arrive(c, k):
        there = zf_s.at[z_of(k), :, c * D : (c + 1) * D]
        remote(there, there, zf_send.at[c, k], zf_recv.at[c, z_of(k)], me, zi).wait_recv()

    def u_block(which, number, count=1):
        width, height = up_s.shape[2] // 4, shard // 2
        columns = pl.ds(pl.multiple_of(chip_of[which] * width, 128), width)
        return zf_s.at[zi, number * height : (number + count) * height, columns]

    def u_copy(slot):
        which, number, target = (
            ("above", 0, above), ("corner", 0, above), ("beside", 1, beside), ("corner", 1, beside),
            ("beside", 0, beside), ("above", 1, above),
        )[slot]
        dst = two1.at[slot] if slot < 4 else three1.at[slot - 4]
        return remote(u_block(which, number), dst, b_send.at[1, slot], b_recv.at[1, slot], target, zi)

    def u_first():
        for c in range(2):
            for k in range(1, docs):
                zf_arrive(c, k)
        width = up_s.shape[2] // 4

        @pl.loop(0, 4)
        def _(k):
            columns = pl.ds(pl.multiple_of(k * width, 128), width)
            total = up_s[zi, :, columns].astype(F32)
            for other in range(1, docs):
                total = total + zf_s[z_of(other), :, columns].astype(F32)
            zf_s[zi, :, columns] = total.astype(BF)

        for slot in range(4):
            u_copy(slot).start()

    def u_second():
        for slot in range(4):
            u_copy(slot).wait_recv()
        add_to(u_block("beside", 0), two1.at[1])
        add_to(u_block("above", 1), two1.at[3])
        for slot in (4, 5):
            u_copy(slot).start()
        add_to(u_block("me", 0), two1.at[0])
        add_to(u_block("me", 1), two1.at[2])

    def target_piece(j, owner):
        if j == 0:
            return piece(KINDS[0], out_sum, 0, 1, owner).at[0]
        if j == 2:
            return down_sum.at[0, lax.rem(owner, 2), lax.div(owner, 2)]
        width = up_sum.shape[2] // 8
        return up_sum.at[0, :, pl.ds(pl.multiple_of(owner * width, 128), width)]

    def p_own(j):
        return pltpu.make_async_copy(fin[j], target_piece(j, me), keep_sem.at[j])

    def p_copy(j, slot, owner=None):
        src = fin[j] if slot in (0, 1, 3) else target_piece(j, owner)
        owner = me if slot in (0, 1, 3) else owner
        target = (beside, above, above if j == 2 else beside, sibling, sibling, sibling, sibling)[slot]
        return remote(src, target_piece(j, owner), p_send.at[j, slot], p_recv.at[j, slot], target, zi)

    def p_pass(j):
        return beside if j == 2 else above

    def p_arrive(j, slot):
        owner = (beside, above, corner, sibling, flip(beside, 1), flip(above, 1), flip(corner, 1))[slot]
        there = target_piece(j, owner)
        remote(there, there, p_send.at[j, slot], p_recv.at[j, slot], sibling, zi).wait_recv()

    def p_start(j):
        if j == 1:
            for slot in (4, 5):
                u_copy(slot).wait_recv()
            total = u_block("me", 0, 2)[...].astype(F32) + three1[...].astype(F32).reshape(fin1.shape)
        else:
            for k in range(1, docs):
                z_arrival(j, k).wait_recv()
            total = acc(j, chip, zi).at[0][...].astype(F32)
            for k in range(1, docs):
                total = total + four[j][lax.rem(zi + k, docs)].astype(F32)
        sq_s[j] = jnp.full(sq_s.shape[1:], jnp.sum(total * total), F32)
        fin[j][...] = total.astype(BF)
        p_own(j).start()
        for slot in (0, 1, 3):
            p_copy(j, slot).start()

    def p_second(j):
        p_arrive(j, 0)
        p_arrive(j, 1)
        p_copy(j, 2, p_pass(j)).start()
        p_copy(j, 4, beside).start()
        p_copy(j, 5, above).start()

    def p_third(j):
        p_arrive(j, 2)
        p_copy(j, 6, corner).start()

    shard = D // docs
    side = shard // 2

    def dw_half(which):
        return pl.ds(pl.multiple_of(which * side, 16), side)

    def dw_copy(h):
        src = dw_s.at[:, dw_half(1 - up_bit), :]
        return remote(src, dwr_s.at[h], w_send.at[h, 0], w_recv.at[h, docs], above, zi)

    def dwz_copy(h, k):
        z = lax.rem(zi + k, docs)
        return remote(dwr_s.at[h, z], dwz_s.at[h, zi], w_send.at[h, k], w_recv.at[h, zi], me, z)

    def dwz_arrival(h, k):
        z = lax.rem(zi + k, docs)
        return remote(dwz_s.at[h, z], dwz_s.at[h, z], w_send.at[h, 0], w_recv.at[h, z], me, z)

    def q_own(h):
        return pltpu.make_async_copy(dwf_s.at[h], qkv_sum.at[me, h], keep_sem.at[3 + h])

    def q_copy(h, slot, owner=None):
        own = slot in (0, 1, 3)
        src = dwf_s.at[h] if own else qkv_sum.at[owner, h]
        target = (beside, above, (above, beside)[h % 2], sibling, sibling, sibling, sibling)[slot]
        return remote(src, qkv_sum.at[me if own else owner, h], q_send.at[h, slot], q_recv.at[h, slot], target, zi)

    def q_pass(h):
        return (beside, above)[h % 2]

    def q_arrive(h, slot):
        owner = (beside, above, corner, sibling, flip(beside, 1), flip(above, 1), flip(corner, 1))[slot]
        there = qkv_sum.at[owner, h]
        remote(there, there, q_send.at[h, slot], q_recv.at[h, slot], sibling, zi).wait_recv()

    def dw_start(h):
        if h == 0:
            load(8).wait()
        else:
            dw_copy(h - 1).wait_send()
        mine = jnp.concatenate([dqkv_s[(p * hp + h) * DH : (p * hp + h + 1) * DH, :] for p in range(3)], axis=0)
        dw = dot(mine, attn_s[...]).T
        for z in range(docs):
            dw_s[z] = dw[z * shard : (z + 1) * shard, :].astype(BF)
        dw_copy(h).start()

    def dw_mid(h):
        dw_copy(h).wait_recv()
        for z in range(docs):
            dwr_s[h, z] = (dwr_s[h, z].astype(F32) + dw_s[z, dw_half(up_bit), :].astype(F32)).astype(BF)
        for k in range(1, docs):
            dwz_copy(h, k).start()

    def dw_end(h):
        for k in range(1, docs):
            dwz_arrival(h, k).wait_recv()
        total = dwr_s[h, zi].astype(F32)
        for k in range(1, docs):
            total = total + dwz_s[h, lax.rem(zi + k, docs)].astype(F32)
        sq_s[3] += jnp.full(sq_s.shape[1:], jnp.sum(total * total), F32)
        dwf_s[h] = total.astype(BF)
        q_own(h).start()
        for slot in (0, 1, 3):
            q_copy(h, slot).start()

    def dw_second(h):
        q_arrive(h, 0)
        q_arrive(h, 1)
        q_copy(h, 2, q_pass(h)).start()
        q_copy(h, 4, beside).start()
        q_copy(h, 5, above).start()

    def dw_third(h):
        q_arrive(h, 2)
        q_copy(h, 6, corner).start()

    def plane_copy(k):
        return remote(plane_s.at[me], plane_s.at[me], plane_send.at[k], plane_recv.at[me], lax.rem(me + k, n), zi)

    def plane_arrival(k):
        owner = lax.rem(me + k, n)
        return remote(plane_s.at[owner], plane_s.at[owner], plane_send.at[0], plane_recv.at[owner], owner, zi)

    def column_copy(k):
        return remote(column_s.at[zi], column_s.at[zi], column_send.at[k], column_recv.at[zi], me, lax.rem(zi + k, docs))

    def column_arrival(k):
        z = lax.rem(zi + k, docs)
        return remote(column_s.at[z], column_s.at[z], column_send.at[0], column_recv.at[z], me, z)

    def tiny_copy(k):
        return remote(tinyp_s.at[me], tinyp_s.at[me], tp_send.at[k], tp_recv.at[me], lax.rem(me + k, n), zi)

    def tiny_arrival(k):
        owner = lax.rem(me + k, n)
        return remote(tinyp_s.at[owner], tinyp_s.at[owner], tp_send.at[0], tp_recv.at[owner], owner, zi)

    def tinyc_copy(k):
        return remote(tinyc_s.at[zi], tinyc_s.at[zi], tc_send.at[k], tc_recv.at[zi], me, lax.rem(zi + k, docs))

    def tinyc_arrival(k):
        z = lax.rem(zi + k, docs)
        return remote(tinyc_s.at[z], tinyc_s.at[z], tc_send.at[0], tc_recv.at[z], me, z)

    pairs = (
        (mixed_ref, mixed_s), (out_all, out_s), (tokens_ref, tokens_s), (out_grad_ref, grad_s), (up_all, up_s),
        (down_all, down_s), (qkv_ref, qkv_s), (of_ref, of_s), (attn_ref, attn_s), (w_ref, w_s),
    )

    def load(number):
        return pltpu.make_async_copy(*pairs[number], load_sem.at[number])

    greet_signal(n, docs)
    for number in range(len(pairs)):
        load(number).start()
    sq_s[...] = jnp.zeros_like(sq_s)
    rows_s[...] = jnp.zeros_like(rows_s)

    def f_copy(number):
        src, dst = (
            (pair_s.at[0:2], pair_s.at[2:4]), (ffn_s.at[0:2], ffn_s.at[2:4]), (tmp_s.at[2:4], dxr_s.at[2:4]),
            (tmp_s.at[0:2], dxr_s.at[0:2]),
        )[number]
        return remote(src, dst, f_send.at[number], f_recv.at[number], sibling, zi)

    lane = lax.broadcasted_iota(jnp.int32, (8, rows), 1)
    place = me * rows + lane
    count_of = count_ref[...]
    terms, kept_of = [], []
    load(3).wait()
    for b in range(batches):
        term = jnp.zeros((1, D), F32)
        for g in range(pool_grad_ref.shape[0]):
            term = jnp.where(group_ref[b] == g, pool_grad_ref[g : g + 1, :] / count_of[0:1, g : g + 1], term)
        kept = jnp.logical_and(place < len_ref[b], mask_ref[b : b + 1, :] == 0).astype(F32)
        terms.append(term)
        kept_of.append(kept.T[:, 0:1])
        pair_s[b] = (grad_s[b].astype(F32) + kept_of[b] * terms[b]).astype(BF)
    greet_wait(n, docs)
    f_copy(0).start()
    for number in range(3):
        load(number).wait()
    out_matrix = out_s[...].reshape(D, D)
    gain_ffn = gain_ref[1:2, :]
    for b in range(batches):
        hidden = tokens_s[b].astype(F32) + dot(mixed_s[b].T, out_matrix)
        hidden_s[b] = hidden
        scale = lax.rsqrt(jnp.mean(hidden * hidden, axis=-1, keepdims=True) + EPS)
        ffn_s[b] = (hidden * scale * gain_ffn).astype(BF)
    f_copy(1).start()
    load(4).wait()
    load(5).wait()
    all_rows = batches * rows
    wide = (all_rows, D)
    each = (batches, rows, D)

    def spread(ref, value):
        for g in range(all_rows // 128):
            ref[:, g * D : (g + 1) * D] = value[g * 128 : (g + 1) * 128, :]

    def gathered(ref):
        return jnp.concatenate([ref[:, g * D : (g + 1) * D] for g in range(all_rows // 128)], axis=0)

    def units(c):
        return up_s[:, :, c * D : (c + 1) * D].reshape(D, D), down_s[c * half : (c + 1) * half].reshape(D, D)

    def through(c, mine):
        here = slice(0, 2) if mine else slice(2, 4)
        ffn_in, grad_ffn = ffn_s[here].reshape(wide), pair_s[here].reshape(wide)
        up_part, down_part = units(c)
        upper = dot(ffn_in, up_part)
        square = upper * upper
        bend = jnp.tanh(CURVE * (upper + CUBIC * upper * square))
        active_s[c, here] = (0.5 * upper * (1.0 + bend)).astype(BF).reshape(each)
        slope = 0.5 * (1.0 + bend) + (0.5 * CURVE) * upper * (1.0 - bend * bend) * (1.0 + (3.0 * CUBIC) * square)
        spread(t_ref, slope)
        upper_s[c, here] = (turned(grad_ffn, down_part) * gathered(t_ref)).astype(BF).reshape(each)
        active, grad_upper = active_s[c, here].reshape(wide), upper_s[c, here].reshape(wide)
        return dot(active, down_part), turned(grad_upper, up_part)

    both = (2 * all_rows, D)

    def half_grads(c):
        down_grad = dot(active_s[c].reshape(both).T, pair_s[...].reshape(both))
        down_s[c * half : (c + 1) * half] = down_grad.astype(BF).reshape(half, *down_s.shape[1:])
        up_grad = dot(ffn_s[...].reshape(both).T, upper_s[c].reshape(both))
        up_s[:, :, c * D : (c + 1) * D] = up_grad.astype(BF).reshape(docs, shard, D)
        for k in range(1, docs):
            zf_copy(c, k).start()

    def half_start(c):
        for slot in (2 * c, 2 * c + 1):
            b_copy(2, slot).start()

    for c in range(2):
        final, back_in = through(c, True)
        final_s[...] = (hidden_s[...] if c == 0 else final_s[...]) + final.reshape(each)
        spread(dt_ref, back_in if c == 0 else gathered(dt_ref) + back_in)
    f_copy(0).wait_recv()
    f_copy(1).wait_recv()
    firsts = through(0, False)
    final, back_in = (first + second for first, second in zip(firsts, through(1, False)))
    tmp_s[2:4] = back_in.astype(BF).reshape(each)
    f_copy(2).start()
    tmp_s[0:2] = final.astype(BF).reshape(each)
    f_copy(3).start()
    half_grads(0)

    index = lax.broadcasted_iota(jnp.int32, (8, D), 0)
    f_copy(2).wait_recv()
    for b in range(batches):
        hidden = hidden_s[b]
        scale = lax.rsqrt(jnp.mean(hidden * hidden, axis=-1, keepdims=True) + EPS)
        unit = hidden * scale
        grad = gathered(dt_ref)[b * rows : (b + 1) * rows, :] + dxr_s[2 + b].astype(F32)
        weighted = grad * gain_ffn
        mean = jnp.mean(weighted * unit, axis=-1, keepdims=True)
        rows_s[...] += jnp.where(index == 1, jnp.sum(grad * unit, axis=0, keepdims=True), 0.0)
        grad_hidden = grad_s[b].astype(F32) + kept_of[b] * terms[b] + scale * (weighted - unit * mean)
        hidden_s[b] = grad_hidden
        active_s[0, b] = grad_hidden.astype(BF)
        gm_s[b] = turned(out_matrix, active_s[0, b]).astype(BF)
    for h in range(hp):
        mix_keep(h).start()
        for k in range(1, n):
            mix_copy(h, k).start()
    out_s[...] = (dot(mixed_s[0], active_s[0, 0]) + dot(mixed_s[1], active_s[0, 1])).astype(BF).reshape(out_s.shape)
    half_grads(1)
    half_start(0)
    half_start(1)
    f_copy(3).wait_recv()
    for b in range(batches):
        final = final_s[b] + dxr_s[b].astype(F32)
        pooled = jnp.sum(kept_of[b] * final, axis=0, keepdims=True)
        rows_s[...] += jnp.where(index == 2 + group_ref[b], pooled, 0.0)
        active_s[0, 2 + b] = final.astype(BF)
    keep_layer = pltpu.make_async_copy(active_s.at[0, 2:4], layer_ref, keep_sem.at[6])
    keep_layer.start()
    for k in range(4):
        a_copy(k).start()
    for number in (6, 7):
        load(number).wait()

    qb = rows
    kc = 512
    blocks = size // qb
    my_length = len_ref[my_doc]

    @pl.loop(0, hp * blocks)
    def _(t):
        h, i = lax.div(t, blocks), lax.rem(t, blocks)
        mine_rows = pl.ds(pl.multiple_of(h * DH, DH), DH)
        key_rows = pl.ds(pl.multiple_of((hp + h) * DH, DH), DH)
        value_rows = pl.ds(pl.multiple_of((2 * hp + h) * DH, DH), DH)

        @pl.when(i == 0)
        def _():
            first = strip_ref[h]
            for step in range(16):
                t_ref[8 * step : 8 * step + 8, :] = pltpu.roll(first, 8 * step, 1) if step else first
            place = lax.broadcasted_iota(jnp.int32, (1, size), 1)
            masked = jnp.where(place < my_length, 0.0, NEG)
            ones = jnp.ones((1, size), F32)
            ka_ref[...] = jnp.concatenate(
                [qkv_s[key_rows, :], extra_rows([masked, ones, ones, ones], size)], axis=0
            ).T
            va_ref[...] = jnp.concatenate(
                [qkv_s[value_rows, :], extra_rows([ones, ones, ones], size)], axis=0
            ).T
            dt_ref[...] = jnp.zeros_like(dt_ref)
            dka_ref[...] = jnp.zeros_like(dka_ref)
            dva_ref[...] = jnp.zeros_like(dva_ref)
            mix_keep(h).wait()
            for k in range(1, n):
                mix_arrival(h, k).wait_recv()

        for when, what in (
            (3, b_first),
            (6, lambda: b_second(2)),
            (8, lambda: (dw_start(0), b_second(0))),
            (12, lambda: (dw_mid(0), z_start(2))),
            (13, lambda: z_start(0)),
            (14, u_first),
            (16, lambda: dw_start(1)),
            (17, lambda: (dw_end(0), u_second())),
            (19, lambda: p_start(2)),
            (20, lambda: (dw_mid(1), p_start(1))),
            (21, lambda: (dw_second(0), p_start(0))),
            (22, lambda: p_second(2)),
            (23, lambda: (dw_end(1), dw_third(0))),
        ):

            @pl.when(t == when)
            def _(what=what):
                what()

        here = pl.ds(pl.multiple_of(i * qb, qb), qb)
        ones = jnp.ones((1, qb), F32)
        q_block = qkv_s[mine_rows, here]
        grad = do_s[mine_rows, here]
        delta = jnp.sum(grad.astype(F32) * of_s[mine_rows, here], axis=0, keepdims=True)
        lse = lse_ref[pl.ds(h, 1), :, here].reshape(1, qb)
        query = jnp.concatenate([q_block, extra_rows([ones, *three(-lse)], qb)], axis=0)
        grad_t = jnp.concatenate([grad, extra_rows([*three(-delta)], qb)], axis=0)
        dq = jnp.zeros((DH, qb), F32)
        held = jnp.zeros((128, qb), F32)

        for c in range(size // kc):
            part_rows = slice(c * kc, (c + 1) * kc)
            s_all, dp_all = dot(ka_ref[part_rows, :], query), dot(va_ref[part_rows, :], grad_t)
            probs, scores = [], []
            for b in range(kc // 128):
                block = c * (kc // 128) + b
                sub = slice(b * 128, (b + 1) * 128)
                start = pl.multiple_of(i * qb + size - 128 - block * 128, 128)
                p = jnp.exp(s_all[sub, :] + t_ref[:, pl.ds(start, qb)])
                ds = p * dp_all[sub, :]
                held = (
                    ds
                    if block == 0
                    else jnp.concatenate([ds[:, :128], held[:, : qb - 128] + ds[:, 128:]], axis=1)
                )
                top = pl.multiple_of(start + qb - 128, 128)
                dt_ref[:, pl.ds(top, 128)] += held[:, qb - 128 :]
                probs.append(p.astype(BF))
                scores.append(ds.astype(BF))
            probs = jnp.concatenate(probs, axis=0)
            scores = jnp.concatenate(scores, axis=0)
            dva_ref[:, part_rows] += turned(grad, probs)
            dka_ref[:, part_rows] += turned(q_block, scores)
            dq = dq + dot(qkv_s[key_rows, part_rows], scores)
        for a in range(qb // 128 - 1):
            start = pl.multiple_of(i * qb + a * 128, 128)
            dt_ref[:, pl.ds(start, 128)] += held[:, a * 128 : (a + 1) * 128]
        dqkv_s[mine_rows, here] = dq.astype(BF)

        @pl.when(i == blocks - 1)
        def _():
            dqkv_s[key_rows, :] = dka_ref[...].astype(BF)
            dqkv_s[value_rows, :] = dva_ref[...].astype(BF)
            total = dt_ref[0:8, :]
            for step in range(1, 16):
                total = total + pltpu.roll(dt_ref[8 * step : 8 * step + 8, :], 2 * size - 8 * step, 1)
            ids = ids_ref[...]
            lane = lax.broadcasted_iota(jnp.int32, (8, D), 1)
            line = lax.broadcasted_iota(jnp.int32, (8, D), 0)
            table = jnp.zeros((8, D), F32)
            for b in range(NB):
                value = jnp.sum(jnp.where(ids == b, total, 0.0))
                mine = jnp.logical_and(lane == (b // 8) * 128 + my_heads * hp + h, line == b % 8)
                table = jnp.where(mine, value, table)
            sq_s[4] += table

    load(9).wait()
    for number in range(4):
        f_copy(number).wait_send()
    keep_layer.wait()
    squares = sq_s[0, 0:1, :] + sq_s[1, 0:1, :] + sq_s[2, 0:1, :] + sq_s[3, 0:1, :]
    plane_s[me, 0:8, :] = jnp.where(index == 7, squares, rows_s[...])
    plane_s[me, 8:16, :] = sq_s[4]
    sq_s[3] = jnp.zeros(sq_s.shape[1:], F32)

    def dx_block(owner):
        here = pl.ds(pl.multiple_of(owner * rows, rows), rows)
        return dot(w_s[...], dqkv_s[:, here]).T

    def dxs_copy(k):
        return remote(tmp_s.at[k], dxr_s.at[k], x_send.at[k], x_recv.at[k], sibling, zi)

    def dxo_copy(k):
        return remote(pair_s.at[k], dxi_s.at[chip], x_send.at[4 + k], x_recv.at[4 + chip], 2 * k + core, zi)

    def dxo_arrival(k):
        return remote(dxi_s.at[k], dxi_s.at[k], x_send.at[0], x_recv.at[4 + k], 2 * k + core, zi)

    order_of = [chip_of[which] for which in ("corner", "beside", "above", "me")]
    for k in order_of:
        tmp_s[k] = dx_block(2 * k + 1 - core).astype(BF)
        dxs_copy(k).start()
    for slot, k in enumerate(order_of):
        mine = dx_block(2 * k + core)
        dxs_copy(k).wait_recv()
        pair_s[k] = (mine + dxr_s[k].astype(F32)).astype(BF)
        if slot < 3:
            dxo_copy(k).start()

    for k in range(1, n):
        plane_copy(k).start()
    p_second(1)
    p_second(0)
    dw_start(2)
    dw_second(1)
    p_third(2)
    for k in range(1, n):
        plane_arrival(k).wait_recv()
    total = plane_s[0]
    for k in range(1, n):
        total = total + plane_s[k]
    column_s[zi] = total
    for k in range(1, docs):
        column_copy(k).start()
    dw_mid(2)
    p_third(1)
    p_third(0)

    for k in range(4):

        @pl.when(k != chip)
        def _(k=k):
            dxo_arrival(k).wait_recv()

        @pl.when(k == chip)
        def _(k=k):
            dxi_s[k] = pair_s[k]

    gain_grad = jnp.zeros((1, D), F32)
    for b in range(batches):
        grad = (dxi_s[2 * b].astype(F32) + dxi_s[2 * b + 1].astype(F32))
        values = tokens_s[b].astype(F32)
        scale = lax.rsqrt(jnp.mean(values * values, axis=-1, keepdims=True) + EPS)
        unit = values * scale
        weighted = grad * gain_ref[0:1, :]
        mean = jnp.mean(weighted * unit, axis=-1, keepdims=True)
        final_s[b] = hidden_s[b] + scale * (weighted - unit * mean)
        gain_grad = gain_grad + jnp.sum(grad * unit, axis=0, keepdims=True)
    keep_tokens = pltpu.make_async_copy(final_s, tokens_grad_ref, keep_sem.at[7])
    keep_tokens.start()
    dw_end(2)
    dw_third(1)

    mine = [gain_grad[:, k * 128 : (k + 1) * 128] for k in range(D // 128)]
    tinyp_s[me] = jnp.concatenate(
        mine + [sq_s[3, 0:1, 0:128], jnp.zeros((7 - len(mine), 128), F32)], axis=0
    )
    for k in range(1, n):
        tiny_copy(k).start()
    for k in range(1, n):
        tiny_arrival(k).wait_recv()
    total = tinyp_s[0]
    for k in range(1, n):
        total = total + tinyp_s[k]
    tinyc_s[zi] = total
    for k in range(1, docs):
        tinyc_copy(k).start()
    dw_second(2)
    for k in range(1, docs):
        column_arrival(k).wait_recv()
    total = column_s[0]
    for z in range(1, docs):
        total = total + column_s[z]
    for k in range(1, docs):
        tinyc_arrival(k).wait_recv()
    tiny = tinyc_s[0]
    for z in range(1, docs):
        tiny = tiny + tinyc_s[z]
    dw_third(2)
    first = jnp.concatenate([tiny[k : k + 1, :] for k in range(D // 128)], axis=1)
    square = jnp.broadcast_to(tiny[D // 128 : D // 128 + 1, 0:1], (1, D))
    vec_out[0:8, :] = jnp.where(index == 0, first, total[0:8, :]) + jnp.where(index == 7, square, 0.0)
    vec_out[8:16, :] = total[8:16, :]

    for slot in (3, 4, 5, 6):
        for j in range(3):
            p_arrive(j, slot)
        for h in range(hp):
            q_arrive(h, slot)
    for h in range(hp):
        q_own(h).wait()
        for k in range(1, docs):
            dwz_copy(h, k).wait_send()
        for slot in range(7):
            q_copy(h, slot, (me, me, q_pass(h), me, beside, above, corner)[slot]).wait_send()
    for j in range(3):
        p_own(j).wait()
        for slot in range(7):
            p_copy(j, slot, (me, me, p_pass(j), me, beside, above, corner)[slot]).wait_send()
        for slot in range(6):
            (u_copy(slot) if j == 1 else b_copy(j, slot)).wait_send()
        for k in range(1, docs):
            if j == 1:
                zf_copy(0, k).wait_send()
                zf_copy(1, k).wait_send()
            else:
                z_copy(j, k).wait_send()
    for k in range(4):
        a_copy(k).wait_send()
    dw_copy(hp - 1).wait_send()
    for k in range(1, n):
        for h in range(hp):
            mix_copy(h, k).wait_send()
    for k in range(1, docs):
        column_copy(k).wait_send()
        tinyc_copy(k).wait_send()
    for k in range(1, n):
        plane_copy(k).wait_send()
        tiny_copy(k).wait_send()
    for k in range(4):
        dxs_copy(k).wait_send()

        @pl.when(k != chip)
        def _(k=k):
            dxo_copy(k).wait_send()

    keep_tokens.wait()


def back(lengths, groups, mixed, tokens, out_grad, pool_grad, mask, counts, gains, weights, saved, hp):
    qkv_t, of_t, lse, strip, ids, attn_in, w = saved
    batches, rows, _ = tokens.shape
    size = qkv_t.shape[1]
    width = 3 * hp * DH
    docs, shard, _ = weights[0].shape
    anywhere, vmem = pl.BlockSpec(memory_space=pl.ANY), pl.BlockSpec(memory_space=pltpu.VMEM)
    smem = pl.BlockSpec(memory_space=pltpu.SMEM)
    dma = pltpu.SemaphoreType.DMA
    shape = jax.ShapeDtypeStruct
    pieces = ((shard // 4, D // 2), (shard, weights[1].shape[2] // 4), weights[2].shape[2:])
    sums = ((shard, D), (shard, 2 * weights[1].shape[2]), (2,) + weights[2].shape[1:])

    def buffers(*lead):
        return [pltpu.VMEM(lead + one, BF) for one in pieces]

    def plane_sums(count):
        by_shard = buffers(count, docs // 2)
        return [by_shard[0], pltpu.VMEM((count, pieces[1][0] // 2, pieces[1][1]), BF), by_shard[2]]

    def rows_of(kind, count=batches):
        return pltpu.VMEM((count, rows, D), kind)

    return pl.pallas_call(
        partial(back_kernel, hp),
        out_shape=(
            shape(tokens.shape, BF),
            shape(tokens.shape, F32),
            *(shape((1,) + one, BF) for one in sums),
            shape((8, hp, shard // 2, 3 * DH), BF),
            shape((16, D), F32),
        ),
        in_specs=[smem, smem] + [anywhere] * 3 + [vmem] * 4 + [anywhere] * 5 + [vmem] * 3 + [anywhere] * 2,
        out_specs=(anywhere,) * 6 + (vmem,),
        scratch_shapes=[
            *(pltpu.VMEM(one.shape, BF) for one in weights),
            pltpu.VMEM(mixed.shape, BF),
            pltpu.VMEM(mixed.shape, BF),
            rows_of(BF), rows_of(BF), rows_of(BF, 4), rows_of(BF, 4), rows_of(BF, 4),
            pltpu.VMEM((2, 4, rows, D), BF),
            pltpu.VMEM((2, 4, rows, D), BF),
            rows_of(F32), rows_of(F32),
            pltpu.VMEM((hp * DH, size), BF),
            pltpu.VMEM((width, size), BF),
            pltpu.VMEM((128, 2 * size), F32),
            pltpu.VMEM((128, 2 * size), F32),
            pltpu.VMEM((size, 128), BF),
            pltpu.VMEM((size, 128), BF),
            pltpu.VMEM((DH, size), F32),
            pltpu.VMEM((DH, size), F32),
            pltpu.VMEM((size, D), BF),
            pltpu.VMEM((D, width), BF),
            pltpu.VMEM((width, size), BF),
            pltpu.VMEM((hp * DH, size), F32),
            buffers(4, docs)[0],
            *plane_sums(4),
            *plane_sums(2),
            buffers(docs)[0], buffers(docs)[2],
            pltpu.VMEM(weights[1].shape, BF),
            *buffers(),
            rows_of(BF, 4), rows_of(BF, 4),
            pltpu.VMEM((docs, shard, 3 * DH), BF),
            pltpu.VMEM((hp, docs, shard // 2, 3 * DH), BF),
            pltpu.VMEM((hp, docs, shard // 2, 3 * DH), BF),
            pltpu.VMEM((hp, shard // 2, 3 * DH), BF),
            pltpu.VMEM((8, D), F32),
            pltpu.VMEM((5, 8, D), F32),
            pltpu.VMEM((8, 16, D), F32),
            pltpu.VMEM((docs, 16, D), F32),
            pltpu.VMEM((8, 8, 128), F32),
            pltpu.VMEM((docs, 8, 128), F32),
            dma((10,)),
            dma((hp, 8)), dma((hp, 8)),
            dma((8,)),
            dma((4,)), dma((4,)),
            dma((4,)), dma((4,)),
            dma((3, 6)), dma((3, 6)),
            dma((2, docs)), dma((2, docs)),
            dma((3, docs)), dma((3, docs)),
            dma((3, 7)), dma((3, 7)),
            dma((8,)), dma((8,)),
            dma((hp, docs)), dma((hp, docs + 1)),
            dma((hp, 7)), dma((hp, 7)),
            dma((8,)), dma((8,)),
            dma((docs,)), dma((docs,)),
            dma((8,)), dma((8,)),
            dma((docs,)), dma((docs,)),
        ],
        compiler_params=pltpu.CompilerParams(
            collective_id=1, has_side_effects=True, vmem_limit_bytes=63 << 20
        ),
        name="back",
    )(
        lengths, groups, mixed, tokens, out_grad, pool_grad, mask, counts, gains, *weights,
        qkv_t, of_t, lse, strip, ids, attn_in, w,
    )


def rms_parts(rows):
    scale = lax.rsqrt(jnp.mean(rows * rows, axis=-1, keepdims=True) + EPS)
    return scale, rows * scale


def rms_back(grad, gain, scale, unit):
    weighted = grad * gain
    rows_part = scale * (weighted - unit * jnp.mean(weighted * unit, axis=-1, keepdims=True))
    return rows_part, jnp.sum(grad * unit, axis=tuple(range(grad.ndim - 1)))


def adam_update(gradient, first_state, second_state, weight, rate, decay, clip):
    gradient = gradient * clip
    first_new = BETA_ONE * first_state + (1.0 - BETA_ONE) * gradient
    second_new = BETA_TWO * second_state + (1.0 - BETA_TWO) * gradient * gradient
    fix_first = 1.0 - BETA_ONE**STEP
    fix_second = 1.0 - BETA_TWO**STEP
    moved = first_new / fix_first / (jnp.sqrt(second_new / fix_second) + ADAM_EPS)
    return (first_new, second_new, weight - rate * (moved + decay * weight))


def update_kernel(
    hp, group_count,
    layer_ref, grad_ref, vec_ref, count_ref, g_qkv, g_out, g_up, g_down,
    w_qkv, w_out, w_up, w_down, w_gain, w_table,
    m_qkv, m_out, m_up, m_down, m_gain, m_table,
    v_qkv, v_out, v_up, v_down, v_gain, v_table,
    layer_out, grad_out, pooled_ref, norm_ref,
    mean_qkv, mean_out, mean_up, mean_down, mean_gain, mean_table,
    square_qkv, square_out, square_up, square_down, square_gain, square_table,
    next_qkv, next_out, next_up, next_down, next_gain, next_table,
    clip_s,
):
    step = pl.program_id(0)
    layer_out[...] = layer_ref[...]
    grad_out[...] = grad_ref[...]
    zi = lax.axis_index("docs")
    shard = w_gain.shape[1]

    def update(gradient, refs, rate, decay):
        w, m, v, mean, square, after = refs
        outs = adam_update(gradient, m[...], v[...], w[...], rate, decay, clip_s[0:1, 0:1])
        mean[...], square[...], after[...] = outs

    @pl.when(step == 0)
    def _():
        gains = vec_ref[0:2, :]
        table = vec_ref[8:16, :]
        squares = vec_ref[7, 0] + jnp.sum(gains * gains) + jnp.sum(table * table)
        norm = jnp.sqrt(jnp.full((1, 128), squares, F32))
        norm_ref[...] = norm
        clip_s[...] = CLIP_NORM / jnp.maximum(norm, CLIP_NORM)
        for g in range(group_count):
            pooled_ref[g : g + 1, :] = vec_ref[2 + g : 3 + g, :] / count_ref[0:1, g : g + 1]
        mine = jnp.zeros((2, shard), F32)
        for z in range(vec_ref.shape[1] // shard):
            mine = jnp.where(zi == z, gains[:, z * shard : (z + 1) * shard], mine)
        update(mine, (w_gain, m_gain, v_gain, mean_gain, square_gain, next_gain), RATES[4], DECAYS[4])
        own = vec_ref[8:16, pl.ds(pl.multiple_of(zi * 128, 128), 128)][:, :H]
        update(own, (w_table, m_table, v_table, mean_table, square_table, next_table), RATES[5], DECAYS[5])

    pieces = [g_qkv[0, k, h].astype(F32) for k in range(g_qkv.shape[1]) for h in range(hp)]
    whole = jnp.concatenate([one[:, p * DH : (p + 1) * DH] for p in range(3) for one in pieces], axis=1)
    update(whole, (w_qkv, m_qkv, v_qkv, mean_qkv, square_qkv, next_qkv), RATES[0], DECAYS[0])
    update(g_out[...].astype(F32), (w_out, m_out, v_out, mean_out, square_out, next_out), RATES[1], DECAYS[1])
    update(g_up[...].astype(F32), (w_up, m_up, v_up, mean_up, square_up, next_up), RATES[2], DECAYS[2])
    update(g_down[...].astype(F32), (w_down, m_down, v_down, mean_down, square_down, next_down), RATES[3], DECAYS[3])


def update_all(layer, grad, vec, counts, gradients, weights, firsts, seconds, hp, group_count):
    shard = weights[0].shape[0]
    steps = shard // 32
    half = steps // 2
    passed = [one.reshape(-1, one.shape[2]) for one in (layer, grad)]

    def by_rows(one):
        return pl.BlockSpec((one.shape[0] // steps, one.shape[1]), lambda i: (i, 0))

    def thin(one):
        blocks = one.shape[0] // 128
        return pl.BlockSpec((128, one.shape[1]), lambda i: (jnp.minimum(i, blocks - 1), 0))

    def whole(one):
        return pl.BlockSpec(one.shape, lambda i: (0,) * one.ndim)

    matrices = [by_rows(one) for one in weights[:4]] + [whole(one) for one in weights[4:]]
    g_qkv = gradients[0].reshape(2, -1, *gradients[0].shape[1:])
    shape = jax.ShapeDtypeStruct
    pooled = shape((group_count, vec.shape[1]), F32)
    norm = shape((1, 128), F32)
    like = [shape(one.shape, F32) for one in weights]
    out = pl.pallas_call(
        partial(update_kernel, hp, group_count),
        grid=(steps,),
        out_shape=(*(shape(one.shape, one.dtype) for one in passed), pooled, norm, *like, *like, *like),
        in_specs=[
            *(thin(one) for one in passed),
            whole(vec),
            whole(counts),
            pl.BlockSpec((1, *g_qkv.shape[1:3], 32, g_qkv.shape[4]), lambda i: (i // half, 0, 0, i % half, 0)),
            *(by_rows(one) for one in gradients[1:]),
        ]
        + matrices * 3,
        out_specs=(*(thin(one) for one in passed), whole(pooled), whole(norm), *matrices, *matrices, *matrices),
        scratch_shapes=[pltpu.VMEM((1, 128), F32)],
        compiler_params=pltpu.CompilerParams(vmem_limit_bytes=56 << 20),
        name="update",
    )(*passed, vec, counts, g_qkv, *gradients[1:], *weights, *firsts, *seconds)
    return out[0].reshape(layer.shape), out[1].reshape(grad.shape), out[2], out[3][0, 0], out[4:]


def share_rows(matrix, seq_size, seq_index):
    rows = matrix.shape[0] // seq_size
    return lax.dynamic_slice_in_dim(matrix, seq_index * rows, rows, 0)


def fits(seq_size, docs_size, batches, rows, length, shard, up_width, down_rows, group_count):
    return (
        (seq_size, batches, rows, length) == (8, 2, 256, 2048)
        and H % 4 == 0
        and H // 4 <= 14
        and NB % docs_size == 0
        and shard == 192
        and up_width % 1024 == 0
        and down_rows % 128 == 0
        and D % 256 == 0
        and docs_size == 4
        and group_count <= 5
        and NB // docs_size == 8
        and docs_size * 128 <= D
        and docs_size * shard == D
    )


def local(
    seq_size,
    docs_size,
    tokens,
    out_grad,
    pool_grad,
    doc_lengths,
    prompt_mask,
    doc_groups,
    bucket_ids,
    qkv_proj,
    out_proj,
    up_proj,
    down_proj,
    norm_gains,
    bias_table,
    qkv_first,
    out_first,
    up_first,
    down_first,
    gain_first,
    table_first,
    qkv_second,
    out_second,
    up_second,
    down_second,
    gain_second,
    table_second,
):
    batches, rows, _ = tokens.shape
    length = (bucket_ids.shape[0] + 1) // 2
    group_count = pool_grad.shape[0]
    shard = qkv_proj.shape[0]
    everyone = ("docs", "seq")
    seq_index = lax.axis_index("seq")
    docs_index = lax.axis_index("docs")
    per_doc = seq_size // batches
    hp = -(-H // per_doc)
    padded = hp * per_doc
    my_doc = seq_index // per_doc
    my_heads = seq_index % per_doc

    def gather_all(matrix):
        return lax.all_gather(share_rows(matrix.astype(BF), seq_size, seq_index), everyone, axis=0, tiled=True)

    def my_columns(matrix):
        by_head = matrix.reshape(matrix.shape[0], 3, H, DH)
        if padded != H:
            by_head = jnp.pad(by_head, ((0, 0), (0, 0), (0, padded - H), (0, 0)))
        mine = lax.dynamic_slice_in_dim(by_head, my_heads * hp, hp, 2)
        return mine.reshape(matrix.shape[0], 3 * hp * DH)

    fused = fits(seq_size, docs_size, batches, rows, length, shard, up_proj.shape[1], down_proj.shape[0], group_count)
    positions = seq_index * rows + jnp.arange(rows, dtype=jnp.int32)
    kept = jnp.logical_and(positions[None, :] < doc_lengths[:, None], prompt_mask == 0).astype(F32)
    group_hot = (doc_groups[:, None] == jnp.arange(group_count, dtype=jnp.int32)[None, :]).astype(F32)
    count_part = jnp.sum(group_hot * jnp.sum(kept, axis=1)[:, None], axis=0)
    my_length = lax.dynamic_slice_in_dim(doc_lengths, my_doc, 1, 0)
    back_ids = jnp.concatenate([jnp.flip(bucket_ids), jnp.zeros((1,), jnp.int32)])
    table_mine = lax.dynamic_slice_in_dim(
        jnp.pad(bias_table, ((0, 0), (0, padded - H))).astype(BF), my_heads * hp, hp, 1
    )
    rows_in = tokens.astype(F32)
    if fused:
        (mixed, *saved, out_all, up_all, down_all, gain_rows, count_rows) = front(
            doc_lengths, doc_groups, tokens, prompt_mask, back_ids[None, :], norm_gains.T, bias_table,
            (qkv_proj, out_proj, up_proj, down_proj), hp, docs_size,
        )
        attn_in, qkv_t, mixed_full, log_total, strip, strip_ids, qkv_mine = saved
        layer_out, tokens_grad, out_sum, up_sum, down_sum, qkv_pieces, vec = back(
            doc_lengths, doc_groups, mixed, tokens, out_grad, pool_grad, prompt_mask, count_rows, gain_rows,
            (out_all, up_all, down_all), (qkv_t, mixed_full, log_total, strip, strip_ids, attn_in, qkv_mine), hp,
        )
        layer_out, tokens_grad, pooled, grad_norm, results = update_all(
            layer_out, tokens_grad, vec, count_rows, (qkv_pieces, out_sum[0], up_sum[0], down_sum.reshape(down_proj.shape)),
            (qkv_proj, out_proj, up_proj, down_proj, norm_gains.T, bias_table),
            (qkv_first, out_first, up_first, down_first, gain_first.T, table_first),
            (qkv_second, out_second, up_second, down_second, gain_second.T, table_second),
            hp, group_count,
        )
        results = [one.T if number % 6 == 4 else one for number, one in enumerate(results)]
        return (layer_out, pooled, tokens_grad, grad_norm, *results)

    small = jnp.concatenate([norm_gains.astype(BF).reshape(-1), table_mine.reshape(-1)])
    small = lax.all_gather(small, "docs", axis=0, tiled=False)
    gains_low = small[:, : 2 * shard].reshape(D, 2)
    table_low = small[:, 2 * shard :].reshape(NB, hp)
    gain_attn = gains_low[:, 0].astype(F32)
    gain_ffn = gains_low[:, 1].astype(F32)
    qkv_mine = lax.all_gather(my_columns(qkv_proj).astype(BF), "docs", axis=0, tiled=True)
    tokens_all = lax.all_gather(tokens, "seq", axis=1, tiled=True)
    doc_rows = lax.dynamic_index_in_dim(tokens_all, my_doc, 0, keepdims=False)
    out_matrix = gather_all(out_proj)
    up_matrix = gather_all(up_proj)
    down_matrix = gather_all(down_proj)
    counts = lax.psum(count_part, everyone)
    bucket_hot = (back_ids[None, :] == jnp.arange(NB, dtype=jnp.int32)[:, None]).astype(BF)
    back_bias = jnp.einsum("bh,bw->hw", table_low, bucket_hot, preferred_element_type=F32)
    strip = jnp.stack([jnp.roll(back_bias, r - 127, axis=1) for r in range(8)], axis=1)
    _, doc_unit = rms_parts(doc_rows.astype(F32))
    attn_in = (doc_unit * gain_attn).astype(BF)
    qkv_t = lax.dot_general(
        qkv_mine, attn_in, (((0,), (1,)), ((), ())), preferred_element_type=F32
    ).astype(BF)
    mixed_low, mixed_full, log_total = attention_forward(qkv_t, strip, my_length, hp)
    pool_share = pool_grad / counts[:, None]

    def to_rows(parts):
        pieces = jnp.transpose(parts.reshape(hp * DH, seq_size, rows), (1, 0, 2))
        pieces = lax.all_to_all(pieces, "seq", 0, 0, tiled=True)
        return pieces.reshape(batches, padded * DH, rows)[:, : H * DH]

    def to_heads(parts):
        if padded != H:
            parts = jnp.pad(parts, ((0, 0), (0, (padded - H) * DH), (0, 0)))
        pieces = lax.all_to_all(parts.reshape(seq_size, hp * DH, rows), "seq", 0, 0, tiled=True)
        return jnp.transpose(pieces, (1, 0, 2)).reshape(hp * DH, length)

    mixed_t = to_rows(mixed_low)

    hidden = rows_in + jnp.einsum("bdr,de->bre", mixed_t, out_matrix, preferred_element_type=F32)
    ffn_scale, ffn_unit = rms_parts(hidden)
    ffn_in = (ffn_unit * gain_ffn).astype(BF)
    up_rows = jnp.einsum("bre,ef->brf", ffn_in, up_matrix, preferred_element_type=F32)
    active = jax.nn.gelu(up_rows, approximate=True).astype(BF)
    final = hidden + jnp.einsum("brf,fe->bre", active, down_matrix, preferred_element_type=F32)
    layer_out = final.astype(BF)
    pool_part = jnp.einsum("bg,be->ge", group_hot, jnp.sum(kept[:, :, None] * final, axis=1), precision=HIGH)
    pool_term = jnp.einsum("bg,ge->be", group_hot, pool_share, precision=HIGH)
    grad_final = out_grad.astype(F32) + kept[:, :, None] * pool_term[:, None, :]
    grad_ffn = grad_final.astype(BF)
    down_grad = jnp.einsum("brf,bre->fe", active, grad_ffn, preferred_element_type=F32)
    grad_active = jnp.einsum("bre,fe->brf", grad_ffn, down_matrix, preferred_element_type=F32)
    _, gelu_pull = jax.vjp(partial(jax.nn.gelu, approximate=True), up_rows)
    grad_upper = gelu_pull(grad_active)[0].astype(BF)
    up_grad = jnp.einsum("bre,brf->ef", ffn_in, grad_upper, preferred_element_type=F32)
    grad_ffn_in = jnp.einsum("brf,ef->bre", grad_upper, up_matrix, preferred_element_type=F32)
    hidden_part, gain_ffn_grad = rms_back(grad_ffn_in, gain_ffn, ffn_scale, ffn_unit)
    grad_hidden = grad_final + hidden_part
    grad_attn = grad_hidden.astype(BF)
    out_grad_part = jnp.einsum("bdr,bre->de", mixed_t, grad_attn, preferred_element_type=F32)
    grad_mixed = jnp.einsum("de,bre->bdr", out_matrix, grad_attn, preferred_element_type=F32).astype(BF)

    def reduce_all(gradient):
        mine = lax.psum_scatter(gradient.astype(BF), everyone, scatter_dimension=0, tiled=True)
        return lax.all_gather(mine, "seq", axis=0, tiled=True).astype(F32)

    down_sum = reduce_all(down_grad)
    up_sum = reduce_all(up_grad)
    out_sum = reduce_all(out_grad_part)

    dq, dk, dv, strip_grad = attention_backward(
        qkv_t, strip, my_length, to_heads(grad_mixed), mixed_full, log_total, hp
    )
    grad_qkv_t = jnp.concatenate([dq, dk, dv], axis=0)
    window_grad = sum(jnp.roll(strip_grad[:, r, :], 127 - r, axis=1) for r in range(8))[:, :-1]
    bucket_full = (back_ids[None, :-1] == jnp.arange(NB, dtype=jnp.int32)[:, None]).astype(F32)
    table_part = jnp.einsum("hw,bw->bh", window_grad, bucket_full, precision=HIGH)
    table_part = lax.dynamic_update_slice_in_dim(jnp.zeros((NB, padded), F32), table_part, my_heads * hp, 1)[:, :H]
    rows_part = lax.dot_general(grad_qkv_t, qkv_mine, (((0,), (1,)), ((), ())), preferred_element_type=F32)
    pieces = lax.all_to_all(rows_part.astype(BF).reshape(seq_size, rows, D), "seq", 0, 0, tiled=True)
    grad_attn_in = jnp.sum(pieces.reshape(batches, per_doc, rows, D).astype(F32), axis=1)
    attn_scale, attn_unit = rms_parts(rows_in)
    tokens_part, gain_attn_grad = rms_back(grad_attn_in, gain_attn, attn_scale, attn_unit)
    tokens_grad = grad_hidden + tokens_part

    qkv_part = lax.dot_general(attn_in, grad_qkv_t, (((0,), (1,)), ((), ())), preferred_element_type=F32)
    qkv_part = lax.psum_scatter(qkv_part.astype(BF), "docs", scatter_dimension=0, tiled=True)
    qkv_parts = lax.all_gather(qkv_part, "seq", axis=0, tiled=False).reshape(batches, per_doc, shard, 3, hp, DH)
    qkv_sum = jnp.transpose(jnp.sum(qkv_parts.astype(F32), axis=0), (1, 2, 0, 3, 4))
    qkv_sum = qkv_sum.reshape(shard, 3, padded, DH)[:, :, :H].reshape(shard, 3 * H * DH)

    squares = sum(jnp.sum(total * total) for total in (qkv_sum, out_sum, up_sum, down_sum)) / seq_size
    gains_part = jnp.stack([gain_attn_grad, gain_ffn_grad], axis=1)
    gains_all, table_all, pool_sum, squares = lax.psum((gains_part, table_part, pool_part, squares), everyone)

    squares = squares + jnp.sum(gains_all * gains_all) + jnp.sum(table_all * table_all)
    grad_norm = jnp.sqrt(squares)
    clip = CLIP_NORM / jnp.maximum(grad_norm, CLIP_NORM)
    pooled = pool_sum / counts[:, None]
    gains_sum = lax.dynamic_slice_in_dim(gains_all, docs_index * shard, shard, 0)
    table_rows = bias_table.shape[0]
    table_sum = lax.dynamic_slice_in_dim(table_all, docs_index * table_rows, table_rows, 0)
    states = zip(
        (qkv_sum, out_sum, up_sum, down_sum, gains_sum, table_sum),
        (qkv_first, out_first, up_first, down_first, gain_first, table_first),
        (qkv_second, out_second, up_second, down_second, gain_second, table_second),
        (qkv_proj, out_proj, up_proj, down_proj, norm_gains, bias_table),
        RATES,
        DECAYS,
    )
    results = [
        adam_update(g_item, m_item, v_item, w_item, rate, decay, clip)
        for g_item, m_item, v_item, w_item, rate, decay in states
    ]
    means, squares_new, nexts = zip(*results)
    return (layer_out, pooled, tokens_grad, grad_norm, *means, *squares_new, *nexts)


def solution(mesh):
    tokens_like = P("docs", "seq", None)
    weights_like = P("docs", None)
    return jax.shard_map(
        partial(local, mesh.shape["seq"], mesh.shape["docs"]),
        mesh=mesh,
        in_specs=(tokens_like, tokens_like, P(), P("docs"), P("docs", "seq"), P("docs"), P()) + (weights_like,) * 18,
        out_specs=(tokens_like, P(), tokens_like, P()) + (weights_like,) * 18,
        check_vma=False,
    )
```
